256 devices in a mesh: row: 8 (over z), col: 8 (over x, y_hi), layer: 4 (over y_lo, core).
Axes of the slice: x: 4, y: 4 (y_hi: 2, y_lo: 2; y = y_hi * 2 + y_lo), z: 8, core: 2. Of those that a mesh axis runs over, the one named last changes fastest.
Arguments:
- left_tiles: bfloat16 [8, 4, 8, 3, 256, 256], P('row', 'layer', 'col'), may hold values from 0.0099487305 to 1
- left_slots: int32 [8, 4, 8, 3], P('row', 'layer', 'col'), may hold values from 0 to 8, as said below
- right_tiles: bfloat16 [8, 4, 8, 6, 256, 256], P('row', 'layer', 'col'), may hold values from 0.01 to 10
- right_slots: int32 [8, 4, 8, 6], P('row', 'layer', 'col'), may hold values from 0 to 16, as said below
Outputs:
- inflated: float32 [4096, 8192], P(('row', 'layer'), 'col')
The draws below stay inside these ranges and needn't reach their ends.
Inputs may be any that keep to these rules, and one draw needn't show every extreme that they name: `left_slots`: in each device's list the slots below 8 are distinct tile positions (tile row p // 4, tile column p % 4); the value 2 * 4 marks an unused entry and may stand anywhere in the list. Every tile row of every device's block has a listed tile, and some device uses all 3 entries. `right_slots`: in each device's list the slots below 16 are distinct tile positions (inner tile row p // 4, tile column p % 4); the value 4 * 4 marks an unused entry and may stand anywhere in the list. Every inner tile row of every device's block has a listed tile, and some device uses all 6 entries.
All inputs are finite; a program needn't handle non-finite values.
Results may differ from the reference program's by a relative error of at most 0.0003.
Values may be sent and summed in bfloat16 or wider, within the bound.
A program may use at most 192 MiB of HBM per device.

```python
import math
import jax
import jax.numpy as jnp
from jax import lax

TILE = 256
ROW_DEV = 512
COL_DEV = 1024
ROW_T = 2
COL_T = 4
KA_T = 4
KB_T = 4
CAP_A = 3
CAP_B = 6
K_LAYER = 8192
ROWS = 4096
COLS = 8192
N_ROW = 8
N_COL = 8
N_LAYER = 4


def tile_lists(base_key, devices, grid_rows, grid_cols, capacity):
    key_rank, key_count, key_full, key_shuffle = jax.random.split(base_key, 4)
    scores = jax.random.randint(key_rank, (devices, grid_rows, grid_cols), 0, 1 << 16) * grid_cols + jnp.arange(grid_cols, dtype=jnp.int32)
    chosen = jnp.argsort(scores, axis=2, stable=True).astype(jnp.int32)
    places = jnp.arange(grid_rows, dtype=jnp.int32)[None, :, None] * grid_cols + chosen
    places = jnp.transpose(places, (0, 2, 1)).reshape(devices, grid_rows * grid_cols)[:, :capacity]
    lowest = max(grid_rows, capacity // 2)
    counts = jax.random.randint(key_count, (devices,), lowest, capacity + 1)
    fullest = jax.random.randint(key_full, (), 0, devices)
    counts = jnp.where(jnp.arange(devices, dtype=jnp.int32) == fullest, capacity, counts)
    places = jnp.where(jnp.arange(capacity, dtype=jnp.int32)[None, :] < counts[:, None], places, grid_rows * grid_cols)
    shuffle = jax.random.randint(key_shuffle, (devices, capacity), 0, 1 << 16) * capacity + jnp.arange(capacity, dtype=jnp.int32)
    permuted = jnp.argsort(shuffle, axis=1, stable=True)
    return jnp.take_along_axis(places, permuted, axis=1).astype(jnp.int32)


def draw_left_slots(key, part):
    key = jax.random.fold_in(key, 11)
    listed = tile_lists(key, N_ROW * N_LAYER * N_COL, ROW_T, KA_T, CAP_A)
    return listed.reshape(N_ROW, N_LAYER, N_COL, CAP_A)


def draw_right_slots(key, part):
    key = jax.random.fold_in(key, 12)
    listed = tile_lists(key, N_ROW * N_LAYER * N_COL, KB_T, COL_T, CAP_B)
    return listed.reshape(N_ROW, N_LAYER, N_COL, CAP_B)


def draw_right_tiles(key, part):
    key = jax.random.fold_in(key, 13)
    key_entry, key_scale = jax.random.split(key, 2)
    shape = (N_ROW, N_LAYER, N_COL, CAP_B, TILE, TILE)
    entries = jnp.exp(jax.random.uniform(key_entry, shape, jnp.float32, -4.6, 0.0))
    spread = jax.random.uniform(key_scale, (1, 1, N_COL, 1, 1, TILE), jnp.float32, 0.0, 1.0)
    return (entries * 10.0 ** spread).astype(jnp.bfloat16)


def level_of(stream_key, extent, shards, smallest, high):
    gain, own = 1.0, jax.random.fold_in(stream_key, 6)
    for dim, shards_of in shards:
        steps = jnp.exp(jax.random.uniform(jax.random.fold_in(own, dim), (shards_of,), jnp.float32, smallest / len(shards), high / len(shards)))
        gain = gain * jnp.repeat(steps, extent[dim] // shards_of).reshape([-1 if axis == dim else 1 for axis in range(len(extent))])
    return gain


def setup_inputs(seed: int = 0) -> dict:
    key_list = jax.random.split(jax.random.key(seed), 5)
    return {
        "left_tiles": jnp.clip(jnp.exp(math.log(1.0) - 4.61031033 * jax.random.uniform(key_list[0], (N_ROW, N_LAYER, N_COL, CAP_A, TILE, TILE), jnp.float32) ** level_of(key_list[0], (N_ROW, N_LAYER, N_COL, CAP_A, TILE, TILE), ((0, 8), (1, 4), (2, 8)), -0.2, 0.2)), 0.0099487305, 1.0).astype(jnp.bfloat16),
        "left_slots": draw_left_slots(jax.random.fold_in(key_list[4], 71), 0),
        "right_tiles": draw_right_tiles(jax.random.fold_in(key_list[4], 71), 0),
        "right_slots": draw_right_slots(jax.random.fold_in(key_list[4], 71), 0),
    }


def densify(tile_list, targets, cells):
    onehot = (targets[:, None] == jnp.arange(cells, dtype=jnp.int32)[None, :]).astype(jnp.float32)
    return jnp.einsum("sp,stu->ptu", onehot, tile_list.astype(jnp.float32))


def arrange(tile_grid, grid_rows, grid_cols):
    tile_edge = tile_grid.shape[-1]
    shaped = tile_grid.reshape(grid_rows, grid_cols, tile_edge, tile_edge)
    return shaped.transpose(0, 2, 1, 3).reshape(grid_rows * tile_edge, grid_cols * tile_edge)


def reference(left_tiles, left_slots, right_tiles, right_slots):
    devices = N_ROW * N_LAYER * N_COL
    left_flat = left_tiles.reshape(devices, CAP_A, TILE, TILE)
    right_flat = right_tiles.reshape(devices, CAP_B, TILE, TILE)

    def left_block(packed):
        return arrange(densify(packed[0], packed[1], ROW_T * KA_T), ROW_T, KA_T).astype(jnp.bfloat16)

    def right_block(packed):
        return arrange(densify(packed[0], packed[1], KB_T * COL_T), KB_T, COL_T).astype(jnp.bfloat16)

    left_blocks = lax.map(left_block, (left_flat, left_slots.reshape(devices, CAP_A)))
    right_blocks = lax.map(right_block, (right_flat, right_slots.reshape(devices, CAP_B)))
    slab = left_blocks.reshape(N_ROW, N_LAYER, N_COL, ROW_DEV, KA_T * TILE)
    slab = slab.transpose(0, 3, 1, 2, 4).reshape(ROWS, N_LAYER, K_LAYER)
    network = right_blocks.reshape(N_ROW, N_LAYER, N_COL, KB_T * TILE, COL_DEV)
    network = network.transpose(1, 0, 3, 2, 4).reshape(N_LAYER, K_LAYER, COLS)
    expanded = jnp.zeros((ROWS, COLS), jnp.float32)
    for layer_index in range(N_LAYER):
        expanded = expanded + jnp.dot(slab[:, layer_index, :], network[layer_index], preferred_element_type=jnp.float32)
    squares = expanded * expanded
    totals = jnp.sum(squares, axis=1, keepdims=True)
    return COLS * squares / totals
```

```python
import jax
import jax.numpy as jnp
from jax import lax
from jax.experimental import pallas as pl
from jax.experimental.pallas import tpu as pltpu
from jax.sharding import PartitionSpec as P

MESH = pl.DeviceIdType.MESH
T = 256
H = 128
N = 8
CAP_A, CAP_B = 3, 6
KT = 4
COL_T = 4
ROW_T = 2
COLS = 8192
LANE_A = 64
HALF = CAP_B // 2
FROM_LEFT, FROM_RIGHT = (1, 2, 3), (1, 2, 3)


def kernel(
    lt, ls, rt, rs, out,
    own0, l10, l20, l30, r10, r20, r30, x40,
    own1, l11, l21, l31, r11, r21, r31, x41,
    abuf, adense, bdense, acc, in1, in2, lanes,
    mytab, ztab, ctab, zsm, csm, mytot, ctot,
    zs, zr, as_, ar, tzs, tzr, tcs, tcr, tos, tor, s1s, s1r, s2s, s2r, loc,
):
    row = lax.axis_index("row")
    col = lax.axis_index("col")
    layer = lax.axis_index("layer")
    core, ylo = layer % 2, layer // 2
    pending = []
    own, x4 = (own0, own1), (x40, x41)
    l1, l2, l3 = (l10, l11), (l20, l21), (l30, l31)
    r1, r2, r3 = (r10, r11), (r20, r21), (r30, r31)

    def send(src, dst, ss, rs_, device):
        copy = pltpu.make_async_remote_copy(
            src_ref=src, dst_ref=dst, send_sem=ss, recv_sem=rs_, device_id=device, device_id_type=MESH
        )
        copy.start()
        pending.append(copy)

    def received(dst, rs_, ss):
        pltpu.make_async_remote_copy(
            src_ref=dst, dst_ref=dst, send_sem=ss, recv_sem=rs_, device_id={"row": (row + 1) % N}, device_id_type=MESH
        ).wait_recv()

    core_peer = {"layer": ylo * 2 + (1 - core)}
    y_peer = {"layer": (1 - ylo) * 2 + core}
    peers = [{"row": (row + o) % N} for o in range(1, N)]
    peers += [{"col": (col + o) % N} for o in range(1, N)]
    peers += [core_peer, y_peer]
    barrier = pltpu.get_barrier_semaphore()
    for peer in peers:
        pl.semaphore_signal(barrier, inc=1, device_id=peer, device_id_type=MESH)

    local = [pltpu.make_async_copy(lt, abuf.at[col, pl.ds(0, CAP_A)], loc.at[0])]
    for h in range(2):
        local.append(
            pltpu.make_async_copy(rt.at[:, :, pl.ds(h * H, H)], own[h].at[pl.ds(0, CAP_B)], loc.at[1 + h])
        )
    for copy in local:
        copy.start()
    for h in range(2):
        for ref in (own, l1, l2, l3, r1, r2, r3, x4):
            ref[h][CAP_B] = jnp.zeros((T, H), jnp.bfloat16)
    for c in range(N):
        abuf[c, CAP_A] = jnp.zeros((T, T), jnp.bfloat16)

    lane = lax.broadcasted_iota(jnp.int32, (8, 128), 1)
    table = jnp.where(lane < LANE_A, CAP_B, CAP_A)
    for s in range(CAP_B):
        table = jnp.where(lane == rs[s], s, table)
    for s in range(CAP_A):
        table = jnp.where(lane == ls[s] + LANE_A, s, table)
    mytab[...] = table
    ztab[row] = table
    ctab[col] = table

    pl.semaphore_wait(barrier, len(peers))

    right, left = {"row": (row + 1) % N}, {"row": (row + N - 1) % N}
    xright, xleft = {"col": (col + 2) % N}, {"col": (col + N - 2) % N}
    ypair_col = col + 1 - 2 * (col % 2)
    ypair = {"col": ypair_col}

    from_left = [None, l1, l2, l3, x4]
    from_right = [None, r1, r2, r3, x4]

    def z_send_right(h, d, q):
        k = h * 7 + (d - 1) * 2 + q
        piece = pl.ds(q * HALF, HALF)
        src = rt.at[piece, :, pl.ds(h * H, H)] if d == 1 else from_left[d - 1][h].at[piece]
        send(src, from_left[d][h].at[piece], zs.at[0, k], zr.at[0, k], right)

    def z_send_left(h, d, q):
        k = h * 7 + (d - 1) * 2 + q
        piece = pl.ds((1 - q) * HALF, HALF)
        src = rt.at[piece, :, pl.ds(h * H, H)] if d == 1 else from_right[d - 1][h].at[piece]
        send(src, from_right[d][h].at[piece], zs.at[1, k], zr.at[1, k], left)

    def z_step(k):
        h, m = k // 7, k % 7
        d, q = m // 2 + 1, m % 2
        received(from_left[d][h].at[pl.ds(q * HALF, HALF)], zr.at[0, k], zs.at[0, k])
        if d < 3 or (d == 3 and q == 0):
            z_send_right(h, d + 1, q)
        received(from_right[d][h].at[pl.ds((1 - q) * HALF, HALF)], zr.at[1, k], zs.at[1, k])
        if d < 3 or (d == 3 and q == 0):
            z_send_left(h, d + 1, q)
        if h == 0 and m in (5, 6):
            z_send_right(1, 1, m - 5)
            z_send_left(1, 1, m - 5)

    def a_send(i, block, part, device):
        ref = abuf.at[block, pl.ds(0, CAP_A)] if part is None else abuf.at[block, pl.ds(0, CAP_A), pl.ds(part * H, H)]
        send(ref, ref, as_.at[i], ar.at[i], device)

    def a_received(i, block, part):
        ref = abuf.at[block, pl.ds(0, CAP_A)] if part is None else abuf.at[block, pl.ds(0, CAP_A), pl.ds(part * H, H)]
        received(ref, ar.at[i], as_.at[i])

    def a_first(base, block):
        a_send(base, block, None, xright)
        a_send(base + 1, block, None, xleft)

    def a_forward(base, block):
        a_received(base, (block + N - 2) % N, None)
        a_send(base + 2, (block + N - 2) % N, 0, xright)
        a_received(base + 1, (block + 2) % N, None)
        a_send(base + 3, (block + 2) % N, 1, xleft)

    def a_last(base, block):
        a_received(base + 2, (block + 4) % N, 0)
        a_received(base + 3, (block + 4) % N, 1)

    for q in range(2):
        z_send_right(0, 1, q)
        z_send_left(0, 1, q)
    local[0].wait()
    a_send(8, col, None, ypair)
    a_first(0, col)
    for o in range(1, N):
        send(mytab, ztab.at[row], tzs.at[o], tzr.at[o], {"row": (row + o) % N})
        send(mytab, ctab.at[col], tcs.at[o], tcr.at[o], {"col": (col + o) % N})
    acc[...] = jnp.zeros_like(acc)
    lanes[...] = jnp.zeros_like(lanes)
    local[1].wait()
    local[2].wait()

    def tables():
        for o in range(1, N):
            received(ztab.at[(row + N - o) % N], tzr.at[o], tzs.at[o])
            received(ctab.at[(col + N - o) % N], tcr.at[o], tcs.at[o])
        c1 = pltpu.make_async_copy(ztab, zsm, loc.at[3])
        c2 = pltpu.make_async_copy(ctab, csm, loc.at[4])
        c1.start()
        c2.start()
        c1.wait()
        c2.wait()

    def densify_a():
        def body(c, carry):
            for i in range(ROW_T):
                for kk in range(KT):
                    s = csm[c, 0, LANE_A + i * KT + kk]
                    adense[c, pl.ds(i * T, T), pl.ds(kk * T, T)] = abuf[c, s]
            return carry

        lax.fori_loop(0, N, body, 0)

    def compute(h, ref, j, after=None):
        for kk in range(KT):
            for jc in range(COL_T):
                s = zsm[j, 0, kk * COL_T + jc]
                bdense[jc // 2, pl.ds(kk * T, T), pl.ds((jc % 2) * H, H)] = ref[h][s]
        for n in range(2):
            for i in range(ROW_T):
                part = jnp.dot(
                    adense[j, pl.ds(i * T, T)], bdense[n], preferred_element_type=jnp.float32
                )
                acc[h, n, 0, i] += part[:H]
                acc[h, n, 1, i] += part[H:]
            if after is not None:
                after(h, n)

    def layer_send(h, n):
        send(acc.at[h, n, 1 - core], in1.at[h, n], s1s.at[h, n], s1r.at[h, n], core_peer)

    def layer_forward(h, n):
        received(in1.at[h, n], s1r.at[h, n], s1s.at[h, n])
        acc[h, n, core, 1 - ylo] += in1[h, n, 1 - ylo]
        send(acc.at[h, n, core, 1 - ylo], in2.at[h, n], s2s.at[h, n], s2r.at[h, n], y_peer)

    def layer_finish(h, n):
        received(in2.at[h, n], s2r.at[h, n], s2s.at[h, n])
        total = acc[h, n, core, ylo] + in1[h, n, ylo] + in2[h, n]
        squares = total * total
        for u in range(2):
            part = squares[:, u * H : (u + 1) * H]
            out[:, pl.ds((n * 2 + u) * T + h * H, H)] = part
            lanes[...] += part

    def at_left(d):
        return (row + N - d) % N

    def at_right(d):
        return (row + d) % N

    for k in range(14):
        z_step(k)
        if k == 2:
            a_forward(0, col)
        elif k == 3:
            tables()
        elif k == 4:
            a_received(8, ypair_col, None)
            a_first(4, ypair_col)
        elif k == 5:
            a_last(0, col)
        elif k == 6:
            a_forward(4, ypair_col)
        elif k == 8:
            a_last(4, ypair_col)
            densify_a()
            compute(0, own, row)
        elif k == 9:
            compute(0, l1, at_left(1))
            compute(0, r1, at_right(1))
            compute(0, l2, at_left(2))
            compute(0, r2, at_right(2))
        elif k == 10:
            compute(0, l3, at_left(3))
            compute(0, r3, at_right(3))
            compute(0, x4, at_left(4), layer_send)
        elif k == 11:
            layer_forward(0, 0)
            layer_forward(0, 1)
            compute(1, own, row)
            compute(1, l1, at_left(1))
            compute(1, r1, at_right(1))
        elif k == 12:
            layer_finish(0, 0)
            layer_finish(0, 1)
            compute(1, l2, at_left(2))
            compute(1, r2, at_right(2))
            compute(1, l3, at_left(3))
            compute(1, r3, at_right(3))
    compute(1, x4, at_left(4), layer_send)
    layer_forward(1, 0)
    layer_forward(1, 1)
    layer_finish(1, 0)
    layer_finish(1, 1)

    line = jnp.sum(lanes[...].T, axis=0, keepdims=True)
    line = jnp.broadcast_to(line, (8, 128))
    mytot[...] = line
    for o in range(1, N):
        send(mytot, ctot.at[col], tos.at[o], tor.at[o], {"col": (col + o) % N})
    ctot[col] = line
    for o in range(1, N):
        received(ctot.at[(col + N - o) % N], tor.at[o], tos.at[o])
    total = ctot[0]
    for c in range(1, N):
        total += ctot[c]
    scale = jnp.broadcast_to((COLS / total)[0:1], (H, H)).T
    for u in range(8):
        out[:, pl.ds(u * H, H)] *= scale
    for copy in pending:
        copy.wait_send()


def local(left_tiles, left_slots, right_tiles, right_slots):
    bf16, f32, i32 = jnp.bfloat16, jnp.float32, jnp.int32
    dma = pltpu.SemaphoreType.DMA
    block = pltpu.VMEM((CAP_B + 1, T, H), bf16)
    return pl.pallas_call(
        kernel,
        out_shape=jax.ShapeDtypeStruct((H, 1024), f32),
        in_specs=[
            pl.BlockSpec(memory_space=pltpu.VMEM),
            pl.BlockSpec(memory_space=pltpu.SMEM),
            pl.BlockSpec(memory_space=pltpu.VMEM),
            pl.BlockSpec(memory_space=pltpu.SMEM),
        ],
        out_specs=pl.BlockSpec(memory_space=pltpu.VMEM),
        scratch_shapes=[
            *[block] * 16,
            pltpu.VMEM((N, CAP_A + 1, T, T), bf16),
            pltpu.VMEM((N, ROW_T * T, KT * T), bf16),
            pltpu.VMEM((2, KT * T, T), bf16),
            pltpu.VMEM((2, 2, 2, 2, H, T), f32),
            pltpu.VMEM((2, 2, 2, H, T), f32),
            pltpu.VMEM((2, 2, H, T), f32),
            pltpu.VMEM((H, H), f32),
            pltpu.VMEM((8, 128), i32),
            pltpu.VMEM((N, 8, 128), i32),
            pltpu.VMEM((N, 8, 128), i32),
            pltpu.SMEM((N, 8, 128), i32),
            pltpu.SMEM((N, 8, 128), i32),
            pltpu.VMEM((8, 128), f32),
            pltpu.VMEM((N, 8, 128), f32),
            dma((2, 14)), dma((2, 14)),
            dma((9,)), dma((9,)),
            dma((N,)), dma((N,)), dma((N,)), dma((N,)), dma((N,)), dma((N,)),
            dma((2, 2)), dma((2, 2)), dma((2, 2)), dma((2, 2)),
            dma((5,)),
        ],
        compiler_params=pltpu.CompilerParams(
            collective_id=0, has_side_effects=True, vmem_limit_bytes=56 * 1024 * 1024
        ),
        cost_estimate=pl.CostEstimate(flops=8_600_000_000, bytes_accessed=2_000_000, transcendentals=0),
    )(
        left_tiles.reshape(CAP_A, T, T),
        left_slots.reshape(CAP_A),
        right_tiles.reshape(CAP_B, T, T),
        right_slots.reshape(CAP_B),
    )


def solution(mesh):
    return jax.shard_map(
        local,
        mesh=mesh,
        in_specs=(
            P("row", "layer", "col", None, None, None),
            P("row", "layer", "col", None),
            P("row", "layer", "col", None, None, None),
            P("row", "layer", "col", None),
        ),
        out_specs=P(("row", "layer"), "col"),
        check_vma=False,
    )
```

```python
import jax
import jax.numpy as jnp
from jax import lax
from jax.experimental import pallas as pl
from jax.experimental.pallas import tpu as pltpu
from jax.sharding import PartitionSpec as P

MESH = pl.DeviceIdType.MESH
T = 256
H = 128
N = 8
CAP_A, CAP_B = 3, 6
KT = 4
COL_T = 4
ROW_T = 2
COLS = 8192
LANE_A = 64
HALF = CAP_B // 2


def kernel(
    lt, ls, rt, rs, out,
    own0, l10, l20, l30, r10, r20, r30, x40,
    own1, l11, l21, l31, r11, r21, r31, x41,
    abuf, adense, bdense, acc, in1, in2, lanes,
    ztab, ctab, zsm, csm, mytot, ctot,
    zs, zr, as_, ar, tzs, tzr, tcs, tcr, tos, tor, s1s, s1r, s2s, s2r, loc,
):
    row = lax.axis_index("row")
    col = lax.axis_index("col")
    layer = lax.axis_index("layer")
    core, ylo = layer % 2, layer // 2
    pending = []
    own, x4 = (own0, own1), (x40, x41)
    l1, l2, l3 = (l10, l11), (l20, l21), (l30, l31)
    r1, r2, r3 = (r10, r11), (r20, r21), (r30, r31)

    def send(src, dst, ss, rs_, device):
        copy = pltpu.make_async_remote_copy(
            src_ref=src, dst_ref=dst, send_sem=ss, recv_sem=rs_, device_id=device, device_id_type=MESH
        )
        copy.start()
        pending.append(copy)

    def received(dst, rs_, ss):
        pltpu.make_async_remote_copy(
            src_ref=dst, dst_ref=dst, send_sem=ss, recv_sem=rs_, device_id={"row": (row + 1) % N}, device_id_type=MESH
        ).wait_recv()

    core_peer = {"layer": ylo * 2 + (1 - core)}
    y_peer = {"layer": (1 - ylo) * 2 + core}
    right, left = {"row": (row + 1) % N}, {"row": (row + N - 1) % N}
    xright, xleft = {"col": (col + 2) % N}, {"col": (col + N - 2) % N}
    ypair_col = col + 1 - 2 * (col % 2)
    ypair = {"col": ypair_col}
    peers = [right, left, xright, xleft, ypair, core_peer, y_peer]
    barrier = pltpu.get_barrier_semaphore()
    for peer in peers:
        pl.semaphore_signal(barrier, inc=1, device_id=peer, device_id_type=MESH)

    local = [pltpu.make_async_copy(lt, abuf.at[col, pl.ds(0, CAP_A)], loc.at[0])]
    for h in range(2):
        local.append(
            pltpu.make_async_copy(rt.at[:, :, pl.ds(h * H, H)], own[h].at[pl.ds(0, CAP_B)], loc.at[1 + h])
        )
    for copy in local:
        copy.start()
    for h in range(2):
        for ref in (own, l1, l2, l3, r1, r2, r3, x4):
            ref[h][CAP_B] = jnp.zeros((T, H), jnp.bfloat16)
    for c in range(N):
        abuf[c, CAP_A] = jnp.zeros((T, T), jnp.bfloat16)

    lane = lax.broadcasted_iota(jnp.int32, (8, 128), 1)
    table = jnp.where(lane < LANE_A, CAP_B, CAP_A)
    for s in range(CAP_B):
        table = jnp.where(lane == rs[s], s, table)
    for s in range(CAP_A):
        table = jnp.where(lane == ls[s] + LANE_A, s, table)
    ztab[row] = table
    ctab[col] = table

    pl.semaphore_wait(barrier, len(peers))

    from_left = [None, l1, l2, l3, x4]
    from_right = [None, r1, r2, r3, x4]

    def z_send_right(h, d, q):
        k = h * 7 + (d - 1) * 2 + q
        piece = pl.ds(q * HALF, HALF)
        src = rt.at[piece, :, pl.ds(h * H, H)] if d == 1 else from_left[d - 1][h].at[piece]
        send(src, from_left[d][h].at[piece], zs.at[0, k], zr.at[0, k], right)

    def z_send_left(h, d, q):
        k = h * 7 + (d - 1) * 2 + q
        piece = pl.ds((1 - q) * HALF, HALF)
        src = rt.at[piece, :, pl.ds(h * H, H)] if d == 1 else from_right[d - 1][h].at[piece]
        send(src, from_right[d][h].at[piece], zs.at[1, k], zr.at[1, k], left)

    def z_step(k):
        h, m = k // 7, k % 7
        d, q = m // 2 + 1, m % 2
        received(from_left[d][h].at[pl.ds(q * HALF, HALF)], zr.at[0, k], zs.at[0, k])
        if d < 3 or (d == 3 and q == 0):
            z_send_right(h, d + 1, q)
        received(from_right[d][h].at[pl.ds((1 - q) * HALF, HALF)], zr.at[1, k], zs.at[1, k])
        if d < 3 or (d == 3 and q == 0):
            z_send_left(h, d + 1, q)
        if h == 0 and m in (5, 6):
            z_send_right(1, 1, m - 5)
            z_send_left(1, 1, m - 5)

    def z_table(d):
        if d > 1:
            received(ztab.at[(row + N - d + 1) % N], tzr.at[0, d - 1], tzs.at[0, d - 1])
            received(ztab.at[(row + d - 1) % N], tzr.at[1, d - 1], tzs.at[1, d - 1])
        lines = ztab.at[(row + N - d + 1) % N]
        send(lines, lines, tzs.at[0, d], tzr.at[0, d], right)
        if d < 4:
            lines = ztab.at[(row + d - 1) % N]
            send(lines, lines, tzs.at[1, d], tzr.at[1, d], left)

    def a_table(i, block, device):
        send(ctab.at[block], ctab.at[block], tcs.at[i], tcr.at[i], device)

    def a_table_received(i, block):
        received(ctab.at[block], tcr.at[i], tcs.at[i])

    def a_send(i, block, part, device):
        ref = abuf.at[block, pl.ds(0, CAP_A)] if part is None else abuf.at[block, pl.ds(0, CAP_A), pl.ds(part * H, H)]
        send(ref, ref, as_.at[i], ar.at[i], device)

    def a_received(i, block, part):
        ref = abuf.at[block, pl.ds(0, CAP_A)] if part is None else abuf.at[block, pl.ds(0, CAP_A), pl.ds(part * H, H)]
        received(ref, ar.at[i], as_.at[i])

    def a_first(base, block):
        a_send(base, block, None, xright)
        a_send(base + 1, block, None, xleft)
        a_table(base, block, xright)
        a_table(base + 1, block, xleft)

    def a_forward(base, block):
        a_received(base, (block + N - 2) % N, None)
        a_send(base + 2, (block + N - 2) % N, 0, xright)
        a_table_received(base, (block + N - 2) % N)
        a_table(base + 2, (block + N - 2) % N, xright)
        a_received(base + 1, (block + 2) % N, None)
        a_send(base + 3, (block + 2) % N, 1, xleft)
        a_table_received(base + 1, (block + 2) % N)

    def a_last(base, block):
        a_received(base + 2, (block + 4) % N, 0)
        a_received(base + 3, (block + 4) % N, 1)
        a_table_received(base + 2, (block + 4) % N)

    for q in range(2):
        z_send_right(0, 1, q)
        z_send_left(0, 1, q)
    local[0].wait()
    a_send(8, col, None, ypair)
    a_table(8, col, ypair)
    a_first(0, col)
    z_table(1)
    acc[...] = jnp.zeros_like(acc)
    lanes[...] = jnp.zeros_like(lanes)
    local[1].wait()
    local[2].wait()

    def tables():
        received(ztab.at[(row + 4) % N], tzr.at[0, 4], tzs.at[0, 4])
        c1 = pltpu.make_async_copy(ztab, zsm, loc.at[3])
        c2 = pltpu.make_async_copy(ctab, csm, loc.at[4])
        c1.start()
        c2.start()
        c1.wait()
        c2.wait()

    def densify_a():
        def body(c, carry):
            for i in range(ROW_T):
                for kk in range(KT):
                    s = csm[c, 0, LANE_A + i * KT + kk]
                    adense[c, pl.ds(i * T, T), pl.ds(kk * T, T)] = abuf[c, s]
            return carry

        lax.fori_loop(0, N, body, 0)

    def compute(h, ref, j, after=None):
        for kk in range(KT):
            for jc in range(COL_T):
                s = zsm[j, 0, kk * COL_T + jc]
                bdense[jc // 2, pl.ds(kk * T, T), pl.ds((jc % 2) * H, H)] = ref[h][s]
        for n in range(2):
            for i in range(ROW_T):
                part = jnp.dot(
                    adense[j, pl.ds(i * T, T)], bdense[n], preferred_element_type=jnp.float32
                )
                acc[h, n, 0, i] += part[:H]
                acc[h, n, 1, i] += part[H:]
            if after is not None:
                after(h, n)

    def layer_send(h, n):
        send(acc.at[h, n, 1 - core], in1.at[h, n], s1s.at[h, n], s1r.at[h, n], core_peer)

    def layer_forward(h, n):
        received(in1.at[h, n], s1r.at[h, n], s1s.at[h, n])
        acc[h, n, core, 1 - ylo] += in1[h, n, 1 - ylo]
        send(acc.at[h, n, core, 1 - ylo], in2.at[h, n], s2s.at[h, n], s2r.at[h, n], y_peer)

    def layer_finish(h, n):
        received(in2.at[h, n], s2r.at[h, n], s2s.at[h, n])
        total = acc[h, n, core, ylo] + in1[h, n, ylo] + in2[h, n]
        squares = total * total
        for u in range(2):
            part = squares[:, u * H : (u + 1) * H]
            out[:, pl.ds((n * 2 + u) * T + h * H, H)] = part
            lanes[...] += part

    def at_left(d):
        return (row + N - d) % N

    def at_right(d):
        return (row + d) % N

    for k in range(14):
        z_step(k)
        if k == 0:
            z_table(2)
        elif k == 1:
            z_table(3)
        elif k == 2:
            a_forward(0, col)
            z_table(4)
        elif k == 4:
            a_received(8, ypair_col, None)
            a_table_received(8, ypair_col)
            a_first(4, ypair_col)
        elif k == 5:
            a_last(0, col)
        elif k == 6:
            a_forward(4, ypair_col)
        elif k == 8:
            a_last(4, ypair_col)
            tables()
            densify_a()
            compute(0, own, row)
        elif k == 9:
            compute(0, l1, at_left(1))
            compute(0, r1, at_right(1))
            compute(0, l2, at_left(2))
            compute(0, r2, at_right(2))
        elif k == 10:
            compute(0, l3, at_left(3))
            compute(0, r3, at_right(3))
            compute(0, x4, at_left(4), layer_send)
        elif k == 11:
            layer_forward(0, 0)
            layer_forward(0, 1)
            compute(1, own, row)
            compute(1, l1, at_left(1))
            compute(1, r1, at_right(1))
        elif k == 12:
            layer_finish(0, 0)
            layer_finish(0, 1)
            compute(1, l2, at_left(2))
            compute(1, r2, at_right(2))
            compute(1, l3, at_left(3))
            compute(1, r3, at_right(3))
    compute(1, x4, at_left(4), layer_send)
    layer_forward(1, 0)
    layer_forward(1, 1)
    layer_finish(1, 0)
    layer_finish(1, 1)

    line = jnp.sum(lanes[...].T, axis=0, keepdims=True)
    line = jnp.broadcast_to(line, (8, 128))
    mytot[...] = line
    for o in range(1, N):
        send(mytot, ctot.at[col], tos.at[o], tor.at[o], {"col": (col + o) % N})
    ctot[col] = line
    for o in range(1, N):
        received(ctot.at[(col + N - o) % N], tor.at[o], tos.at[o])
    total = ctot[0]
    for c in range(1, N):
        total += ctot[c]
    scale = jnp.broadcast_to((COLS / total)[0:1], (H, H)).T
    for u in range(8):
        out[:, pl.ds(u * H, H)] *= scale
    for copy in pending:
        copy.wait_send()


def local(left_tiles, left_slots, right_tiles, right_slots):
    bf16, f32, i32 = jnp.bfloat16, jnp.float32, jnp.int32
    dma = pltpu.SemaphoreType.DMA
    block = pltpu.VMEM((CAP_B + 1, T, H), bf16)
    return pl.pallas_call(
        kernel,
        out_shape=jax.ShapeDtypeStruct((H, 1024), f32),
        in_specs=[
            pl.BlockSpec(memory_space=pltpu.VMEM),
            pl.BlockSpec(memory_space=pltpu.SMEM),
            pl.BlockSpec(memory_space=pltpu.VMEM),
            pl.BlockSpec(memory_space=pltpu.SMEM),
        ],
        out_specs=pl.BlockSpec(memory_space=pltpu.VMEM),
        scratch_shapes=[
            *[block] * 16,
            pltpu.VMEM((N, CAP_A + 1, T, T), bf16),
            pltpu.VMEM((N, ROW_T * T, KT * T), bf16),
            pltpu.VMEM((2, KT * T, T), bf16),
            pltpu.VMEM((2, 2, 2, 2, H, T), f32),
            pltpu.VMEM((2, 2, 2, H, T), f32),
            pltpu.VMEM((2, 2, H, T), f32),
            pltpu.VMEM((H, H), f32),
            pltpu.VMEM((N, 8, 128), i32),
            pltpu.VMEM((N, 8, 128), i32),
            pltpu.SMEM((N, 8, 128), i32),
            pltpu.SMEM((N, 8, 128), i32),
            pltpu.VMEM((8, 128), f32),
            pltpu.VMEM((N, 8, 128), f32),
            dma((2, 14)), dma((2, 14)),
            dma((9,)), dma((9,)),
            dma((2, 5)), dma((2, 5)), dma((9,)), dma((9,)), dma((N,)), dma((N,)),
            dma((2, 2)), dma((2, 2)), dma((2, 2)), dma((2, 2)),
            dma((5,)),
        ],
        compiler_params=pltpu.CompilerParams(
            collective_id=0, has_side_effects=True, vmem_limit_bytes=56 * 1024 * 1024
        ),
        cost_estimate=pl.CostEstimate(flops=8_600_000_000, bytes_accessed=2_000_000, transcendentals=0),
    )(
        left_tiles.reshape(CAP_A, T, T),
        left_slots.reshape(CAP_A),
        right_tiles.reshape(CAP_B, T, T),
        right_slots.reshape(CAP_B),
    )


def solution(mesh):
    return jax.shard_map(
        local,
        mesh=mesh,
        in_specs=(
            P("row", "layer", "col", None, None, None),
            P("row", "layer", "col", None),
            P("row", "layer", "col", None, None, None),
            P("row", "layer", "col", None),
        ),
        out_specs=P(("row", "layer"), "col"),
        check_vma=False,
    )
```

```python
import jax
import jax.numpy as jnp
from jax import lax
from jax.experimental import pallas as pl
from jax.experimental.pallas import tpu as pltpu
from jax.sharding import PartitionSpec as P

MESH = pl.DeviceIdType.MESH
T = 256
H = 128
N = 8
CAP_A, CAP_B = 3, 6
KT = 4
COL_T = 4
Q = 64
ROW_T = 2
COLS = 8192
SENT_LATER = 24
LANE_A = 64
HALF = CAP_B // 2
ORDER = [(0, 1, 0), (0, 1, 1), (0, 2, 0), (0, 2, 1), (0, 3, 0), (0, 3, 1), (0, 4, 0)]
ORDER += [(1, 1, 0), (1, 1, 1), (2, 1, 0), (1, 2, 0), (1, 2, 1), (2, 1, 1), (1, 3, 0), (1, 3, 1)]
ORDER += [(2, 2, 0), (1, 4, 0), (2, 2, 1), (2, 3, 0), (2, 3, 1), (2, 4, 0)]


def kernel(
    lt, ls, rt, rs, out,
    own0, l10, l20, l30, r10, r20, r30, x40,
    own1, l11, l21, l31, r11, r21, r31, x41,
    own2, l12, l22, l32, r12, r22, r32, x42,
    raw,
    abuf, adense, bdense, bturned, acc, in1, in2, lanes,
    ztab, ctab, zsm, csm, mytot, ctot,
    zs, zr, as_, ar, tzs, tzr, tcs, tcr, tos, tor, s1s, s1r, s2s, s2r, loc,
):
    row = lax.axis_index("row")
    col = lax.axis_index("col")
    layer = lax.axis_index("layer")
    core, ylo = layer % 2, layer // 2
    pending = []
    own, x4 = (own0, own1, own2), (x40, x41, x42)
    l1, l2, l3 = (l10, l11, l12), (l20, l21, l22), (l30, l31, l32)
    r1, r2, r3 = (r10, r11, r12), (r20, r21, r22), (r30, r31, r32)

    def send(src, dst, ss, rs_, device):
        copy = pltpu.make_async_remote_copy(
            src_ref=src, dst_ref=dst, send_sem=ss, recv_sem=rs_, device_id=device, device_id_type=MESH
        )
        copy.start()
        pending.append(copy)

    def sent(count):
        for copy in pending[: max(count, 0)]:
            copy.wait_send()
        del pending[: max(count, 0)]

    def received(dst, rs_, ss):
        pltpu.make_async_remote_copy(
            src_ref=dst, dst_ref=dst, send_sem=ss, recv_sem=rs_, device_id={"row": (row + 1) % N}, device_id_type=MESH
        ).wait_recv()

    core_peer = {"layer": ylo * 2 + (1 - core)}
    y_peer = {"layer": (1 - ylo) * 2 + core}
    right, left = {"row": (row + 1) % N}, {"row": (row + N - 1) % N}
    xright, xleft = {"col": (col + 2) % N}, {"col": (col + N - 2) % N}
    ypair_col = col + 1 - 2 * (col % 2)
    ypair = {"col": ypair_col}
    peers = [right, left, xright, xleft, ypair, core_peer, y_peer]
    barrier = pltpu.get_barrier_semaphore()
    for peer in peers:
        pl.semaphore_signal(barrier, inc=1, device_id=peer, device_id_type=MESH)

    local = [pltpu.make_async_copy(lt, abuf.at[col, pl.ds(0, CAP_A)], loc.at[0])]
    local.append(pltpu.make_async_copy(rt.at[:, :, pl.ds(0, H)], own0.at[pl.ds(0, CAP_B)], loc.at[1]))
    local.append(pltpu.make_async_copy(rt.at[:, :, pl.ds(H, H)], raw, loc.at[2]))
    for copy in local:
        copy.start()
    pl.semaphore_wait(barrier, len(peers))

    from_left = [None, l1, l2, l3, x4]
    from_right = [None, r1, r2, r3, x4]

    def z_send(k):
        p, d, q = ORDER[k]
        for way, (held, device) in enumerate(((from_left, right), (from_right, left))):
            piece = pl.ds((q if way == 0 else 1 - q) * HALF, HALF)
            if d > 1:
                src = held[d - 1][p].at[piece]
            elif p == 0:
                src = rt.at[piece, :, pl.ds(0, H)]
            else:
                src = own[p].at[piece]
            send(src, held[d][p].at[piece], zs.at[way, k], zr.at[way, k], device)

    def z_step(k):
        p, d, q = ORDER[k]
        for way, held in enumerate((from_left, from_right)):
            piece = pl.ds((q if way == 0 else 1 - q) * HALF, HALF)
            received(held[d][p].at[piece], zr.at[way, k], zs.at[way, k])
        while len(started) < len(ORDER):
            j = len(started)
            p, d, q = ORDER[j]
            if j - k > (2 if p == 0 else 3) or (d > 1 and ORDER.index((p, d - 1, q)) > k):
                break
            started.append(j)
            z_send(j)

    def z_table(d):
        if d > 1:
            received(ztab.at[(row + N - d + 1) % N], tzr.at[0, d - 1], tzs.at[0, d - 1])
            received(ztab.at[(row + d - 1) % N], tzr.at[1, d - 1], tzs.at[1, d - 1])
        lines = ztab.at[(row + N - d + 1) % N]
        send(lines, lines, tzs.at[0, d], tzr.at[0, d], right)
        if d < 4:
            lines = ztab.at[(row + d - 1) % N]
            send(lines, lines, tzs.at[1, d], tzr.at[1, d], left)

    def a_table(i, block, device):
        send(ctab.at[block], ctab.at[block], tcs.at[i], tcr.at[i], device)

    def a_table_received(i, block):
        received(ctab.at[block], tcr.at[i], tcs.at[i])

    def a_send(i, block, part, device):
        ref = abuf.at[block, pl.ds(0, CAP_A)] if part is None else abuf.at[block, pl.ds(0, CAP_A), pl.ds(part * H, H)]
        send(ref, ref, as_.at[i], ar.at[i], device)

    def a_received(i, block, part):
        ref = abuf.at[block, pl.ds(0, CAP_A)] if part is None else abuf.at[block, pl.ds(0, CAP_A), pl.ds(part * H, H)]
        received(ref, ar.at[i], as_.at[i])

    def a_first(base, block):
        a_send(base, block, None, xright)
        a_send(base + 1, block, None, xleft)
        a_table(base, block, xright)
        a_table(base + 1, block, xleft)

    def a_forward(base, block):
        a_received(base, (block + N - 2) % N, None)
        a_send(base + 2, (block + N - 2) % N, 0, xright)
        a_table_received(base, (block + N - 2) % N)
        a_table(base + 2, (block + N - 2) % N, xright)
        a_received(base + 1, (block + 2) % N, None)
        a_send(base + 3, (block + 2) % N, 1, xleft)
        a_table_received(base + 1, (block + 2) % N)

    def a_last(base, block):
        a_received(base + 2, (block + 4) % N, 0)
        a_received(base + 3, (block + 4) % N, 1)
        a_table_received(base + 2, (block + 4) % N)

    started = [0, 1]
    z_send(0)
    z_send(1)
    for ref in (own, l1, l2, l3, r1, r2, r3, x4):
        ref[0][CAP_B] = jnp.zeros((T, H), jnp.bfloat16)
        for p in (1, 2):
            ref[p][CAP_B] = jnp.zeros((Q, T), jnp.bfloat16)
    for c in range(N):
        abuf[c, CAP_A] = jnp.zeros((T, T), jnp.bfloat16)

    low = lax.broadcasted_iota(jnp.int32, (H, H), 1) < Q
    lane = lax.broadcasted_iota(jnp.int32, (8, 128), 1)
    table = jnp.where(lane < LANE_A, CAP_B, CAP_A)
    for s in range(CAP_B):
        table = jnp.where(lane == rs[s], s, table)
    for s in range(CAP_A):
        table = jnp.where(lane == ls[s] + LANE_A, s, table)
    ztab[row] = table
    ctab[col] = table
    local[0].wait()
    a_send(8, col, None, ypair)
    a_table(8, col, ypair)
    a_first(0, col)
    z_table(1)
    acc[...] = jnp.zeros_like(acc)
    lanes[...] = jnp.zeros_like(lanes)
    local[1].wait()
    local[2].wait()
    for tile in range(CAP_B):
        turned = raw[tile].T
        own1[tile] = turned[:Q]
        own2[tile] = turned[Q:]

    def tables():
        received(ztab.at[(row + 4) % N], tzr.at[0, 4], tzs.at[0, 4])
        c1 = pltpu.make_async_copy(ztab, zsm, loc.at[3])
        c2 = pltpu.make_async_copy(ctab, csm, loc.at[4])
        c1.start()
        c2.start()
        c1.wait()
        c2.wait()

    def densify_a(first, last):
        def body(c, carry):
            for i in range(ROW_T):
                for kk in range(KT):
                    s = csm[c, 0, LANE_A + i * KT + kk]
                    adense[c, pl.ds(i * T, T), pl.ds(kk * T, T)] = abuf[c, s]
            return carry

        lax.fori_loop(first, last, body, 0)

    def compute(p, ref, j, after=None):
        for kk in range(KT):
            for jc in range(COL_T):
                s = zsm[j, 0, kk * COL_T + jc]
                if p == 0:
                    bdense[jc // 2, pl.ds(kk * T, T), pl.ds((jc % 2) * H, H)] = ref[p][s]
                else:
                    bturned[pl.ds(jc * Q, Q), pl.ds(kk * T, T)] = ref[p][s]
        for n in range(2) if p == 0 else (p + 1,):
            for i in range(ROW_T):
                rows = adense[j, pl.ds(i * T, T)]
                if p == 0:
                    part = jnp.dot(rows, bdense[n], preferred_element_type=jnp.float32)
                else:
                    part = lax.dot_general(
                        rows, bturned[...], (((1,), (1,)), ((), ())), preferred_element_type=jnp.float32
                    )
                acc[n, 0, i] += part[:H]
                acc[n, 1, i] += part[H:]
            if after is not None:
                after(n)

    def layer_send(n):
        send(acc.at[n, 1 - core], in1.at[n], s1s.at[n], s1r.at[n], core_peer)

    def layer_forward(n):
        received(in1.at[n], s1r.at[n], s1s.at[n])
        acc[n, core, 1 - ylo] += in1[n, 1 - ylo]
        send(acc.at[n, core, 1 - ylo], in2.at[n], s2s.at[n], s2r.at[n], y_peer)

    def layer_finish(n):
        received(in2.at[n], s2r.at[n], s2s.at[n])
        total = acc[n, core, ylo] + in1[n, ylo] + in2[n]
        squares = total * total
        lanes[...] += squares[:, :H] + squares[:, H:]
        for u in range(2):
            part = squares[:, u * H : (u + 1) * H]
            if n < 2:
                out[:, pl.ds((n * 2 + u) * T, H)] = part
                continue
            turned = pltpu.roll(part, Q, 1)
            for v in range(2):
                place = pl.ds((u * 2 + v) * T + H, H)
                if n == 2:
                    out[:, place] = turned if v else part
                else:
                    out[:, place] = jnp.where(low, out[:, place], part if v else turned)

    def at_left(d):
        return (row + N - d) % N

    def at_right(d):
        return (row + d) % N

    last = len(ORDER) - 1
    for k in range(last):
        z_step(k)
        if k >= 3:
            sent(len(pending) - SENT_LATER)
        if k == 0:
            z_table(2)
        elif k == 1:
            z_table(3)
        elif k == 2:
            z_table(4)
            a_forward(0, col)
            a_received(8, ypair_col, None)
            a_table_received(8, ypair_col)
            a_first(4, ypair_col)
        elif k == 4:
            a_last(0, col)
        elif k == 5:
            a_forward(4, ypair_col)
        elif k == 8:
            a_last(4, ypair_col)
            tables()
            densify_a(0, N // 2)
        elif k == 9:
            densify_a(N // 2, N)
        elif k == 10:
            compute(0, own, row)
            compute(0, l1, at_left(1))
        elif k == 11:
            compute(0, r1, at_right(1))
            compute(0, l2, at_left(2))
        elif k == 12:
            compute(0, r2, at_right(2))
            compute(0, l3, at_left(3))
        elif k == 13:
            compute(0, r3, at_right(3))
            compute(0, x4, at_left(4), layer_send)
        elif k == 14:
            compute(1, own, row)
            compute(1, l1, at_left(1))
            compute(1, r1, at_right(1))
            layer_forward(0)
            layer_forward(1)
        elif k == 15:
            compute(1, l2, at_left(2))
            compute(1, r2, at_right(2))
            compute(1, l3, at_left(3))
            compute(1, r3, at_right(3))
        elif k == 16:
            compute(1, x4, at_left(4), layer_send)
            compute(2, own, row)
            compute(2, l1, at_left(1))
            compute(2, r1, at_right(1))
        elif k == 17:
            layer_forward(2)
            layer_finish(0)
        elif k == 18:
            layer_finish(1)
            compute(2, l2, at_left(2))
            compute(2, r2, at_right(2))
        elif k == 19:
            compute(2, l3, at_left(3))
            compute(2, r3, at_right(3))
    z_step(last)
    compute(2, x4, at_left(4), layer_send)
    layer_finish(2)
    layer_forward(3)
    layer_finish(3)

    line = jnp.sum(lanes[...].T, axis=0, keepdims=True)
    line = jnp.broadcast_to(line, (8, 128))
    mytot[...] = line
    for o in range(1, N):
        send(mytot, ctot.at[col], tos.at[o], tor.at[o], {"col": (col + o) % N})
    ctot[col] = line
    sent(len(pending) - (N - 1))
    for o in range(1, N):
        received(ctot.at[(col + N - o) % N], tor.at[o], tos.at[o])
    total = ctot[0]
    for c in range(1, N):
        total += ctot[c]
    scale = jnp.broadcast_to((COLS / total)[0:1], (H, H)).T
    for u in range(8):
        out[:, pl.ds(u * H, H)] *= scale
    sent(len(pending))


def local(left_tiles, left_slots, right_tiles, right_slots):
    bf16, f32, i32 = jnp.bfloat16, jnp.float32, jnp.int32
    dma = pltpu.SemaphoreType.DMA
    block = pltpu.VMEM((CAP_B + 1, T, H), bf16)
    turned = pltpu.VMEM((CAP_B + 1, Q, T), bf16)
    return pl.pallas_call(
        kernel,
        out_shape=jax.ShapeDtypeStruct((H, 1024), f32),
        in_specs=[
            pl.BlockSpec(memory_space=pl.ANY),
            pl.BlockSpec(memory_space=pltpu.SMEM),
            pl.BlockSpec(memory_space=pl.ANY),
            pl.BlockSpec(memory_space=pltpu.SMEM),
        ],
        out_specs=pl.BlockSpec(memory_space=pltpu.VMEM),
        scratch_shapes=[
            *[block] * 8,
            *[turned] * 16,
            pltpu.VMEM((CAP_B, T, H), bf16),
            pltpu.VMEM((N, CAP_A + 1, T, T), bf16),
            pltpu.VMEM((N, ROW_T * T, KT * T), bf16),
            pltpu.VMEM((2, KT * T, T), bf16),
            pltpu.VMEM((4 * Q, KT * T), bf16),
            pltpu.VMEM((4, 2, 2, H, T), f32),
            pltpu.VMEM((4, 2, H, T), f32),
            pltpu.VMEM((4, H, T), f32),
            pltpu.VMEM((H, H), f32),
            pltpu.VMEM((N, 8, 128), i32),
            pltpu.VMEM((N, 8, 128), i32),
            pltpu.SMEM((N, 8, 128), i32),
            pltpu.SMEM((N, 8, 128), i32),
            pltpu.VMEM((8, 128), f32),
            pltpu.VMEM((N, 8, 128), f32),
            dma((2, len(ORDER))), dma((2, len(ORDER))),
            dma((9,)), dma((9,)),
            dma((2, 5)), dma((2, 5)), dma((9,)), dma((9,)), dma((N,)), dma((N,)),
            dma((4,)), dma((4,)), dma((4,)), dma((4,)),
            dma((5,)),
        ],
        compiler_params=pltpu.CompilerParams(
            collective_id=0, has_side_effects=True, vmem_limit_bytes=56 * 1024 * 1024
        ),
        cost_estimate=pl.CostEstimate(flops=8_600_000_000, bytes_accessed=2_000_000, transcendentals=0),
    )(
        left_tiles.reshape(CAP_A, T, T),
        left_slots.reshape(CAP_A),
        right_tiles.reshape(CAP_B, T, T),
        right_slots.reshape(CAP_B),
    )


def solution(mesh):
    return jax.shard_map(
        local,
        mesh=mesh,
        in_specs=(
            P("row", "layer", "col", None, None, None),
            P("row", "layer", "col", None),
            P("row", "layer", "col", None, None, None),
            P("row", "layer", "col", None),
        ),
        out_specs=P(("row", "layer"), "col"),
        check_vma=False,
    )
```

```python
import jax
import jax.numpy as jnp
from jax import lax
from jax.experimental import pallas as pl
from jax.experimental.pallas import tpu as pltpu
from jax.sharding import PartitionSpec as P

MESH = pl.DeviceIdType.MESH
T = 256
H = 128
N = 8
CAP_A, CAP_B = 3, 6
KT = 4
COL_T = 4
Q = 64
ROW_T = 2
COLS = 8192
SENT_LATER = 24
LANE_A = 64
HALF = CAP_B // 2
LOWEST, STEPS, ZERO = -6.0, 65534 / 23, -32768
ORDER = [(0, 1, 0), (0, 1, 1), (0, 2, 0), (0, 2, 1), (0, 3, 0), (0, 3, 1), (0, 4, 0)]
ORDER += [(1, 1, 0), (1, 1, 1), (2, 1, 0), (1, 2, 0), (1, 2, 1), (2, 1, 1), (1, 3, 0), (1, 3, 1)]
ORDER += [(2, 2, 0), (1, 4, 0), (2, 2, 1), (2, 3, 0), (2, 3, 1), (2, 4, 0)]


def kernel(
    lt, ls, rt, rs, out,
    own0, l10, l20, l30, r10, r20, r30, x40,
    own1, l11, l21, l31, r11, r21, r31, x41,
    own2, l12, l22, l32, r12, r22, r32, x42,
    raw,
    abuf, adense, bdense, bturned, acc, in1, in2, coded, incoded, lanes,
    ztab, ctab, zsm, csm, mytot, ctot,
    zs, zr, as_, ar, tzs, tzr, tcs, tcr, tos, tor, s1s, s1r, s2s, s2r, loc,
):
    row = lax.axis_index("row")
    col = lax.axis_index("col")
    layer = lax.axis_index("layer")
    core, ylo = layer % 2, layer // 2
    pending = []
    own, x4 = (own0, own1, own2), (x40, x41, x42)
    l1, l2, l3 = (l10, l11, l12), (l20, l21, l22), (l30, l31, l32)
    r1, r2, r3 = (r10, r11, r12), (r20, r21, r22), (r30, r31, r32)

    def send(src, dst, ss, rs_, device):
        copy = pltpu.make_async_remote_copy(
            src_ref=src, dst_ref=dst, send_sem=ss, recv_sem=rs_, device_id=device, device_id_type=MESH
        )
        copy.start()
        pending.append(copy)

    def sent(count):
        for copy in pending[: max(count, 0)]:
            copy.wait_send()
        del pending[: max(count, 0)]

    def received(dst, rs_, ss):
        pltpu.make_async_remote_copy(
            src_ref=dst, dst_ref=dst, send_sem=ss, recv_sem=rs_, device_id={"row": (row + 1) % N}, device_id_type=MESH
        ).wait_recv()

    core_peer = {"layer": ylo * 2 + (1 - core)}
    y_peer = {"layer": (1 - ylo) * 2 + core}
    right, left = {"row": (row + 1) % N}, {"row": (row + N - 1) % N}
    xright, xleft = {"col": (col + 2) % N}, {"col": (col + N - 2) % N}
    ypair_col = col + 1 - 2 * (col % 2)
    ypair = {"col": ypair_col}
    peers = [right, left, xright, xleft, ypair, core_peer, y_peer]
    barrier = pltpu.get_barrier_semaphore()
    for peer in peers:
        pl.semaphore_signal(barrier, inc=1, device_id=peer, device_id_type=MESH)

    local = [pltpu.make_async_copy(lt, abuf.at[col, pl.ds(0, CAP_A)], loc.at[0])]
    local.append(pltpu.make_async_copy(rt.at[:, :, pl.ds(0, H)], own0.at[pl.ds(0, CAP_B)], loc.at[1]))
    local.append(pltpu.make_async_copy(rt.at[:, :, pl.ds(H, H)], raw, loc.at[2]))
    for copy in local:
        copy.start()
    pl.semaphore_wait(barrier, len(peers))

    from_left = [None, l1, l2, l3, x4]
    from_right = [None, r1, r2, r3, x4]

    def z_send(k):
        p, d, q = ORDER[k]
        for way, (held, device) in enumerate(((from_left, right), (from_right, left))):
            piece = pl.ds((q if way == 0 else 1 - q) * HALF, HALF)
            if d > 1:
                src = held[d - 1][p].at[piece]
            elif p == 0:
                src = rt.at[piece, :, pl.ds(0, H)]
            else:
                src = own[p].at[piece]
            send(src, held[d][p].at[piece], zs.at[way, k], zr.at[way, k], device)

    def z_step(k):
        p, d, q = ORDER[k]
        for way, held in enumerate((from_left, from_right)):
            piece = pl.ds((q if way == 0 else 1 - q) * HALF, HALF)
            received(held[d][p].at[piece], zr.at[way, k], zs.at[way, k])
        while len(started) < len(ORDER):
            j = len(started)
            p, d, q = ORDER[j]
            if j - k > (2 if p == 0 else 4) or (d > 1 and ORDER.index((p, d - 1, q)) > k):
                break
            started.append(j)
            z_send(j)

    def z_table(d):
        if d > 1:
            received(ztab.at[(row + N - d + 1) % N], tzr.at[0, d - 1], tzs.at[0, d - 1])
            received(ztab.at[(row + d - 1) % N], tzr.at[1, d - 1], tzs.at[1, d - 1])
        lines = ztab.at[(row + N - d + 1) % N]
        send(lines, lines, tzs.at[0, d], tzr.at[0, d], right)
        if d < 4:
            lines = ztab.at[(row + d - 1) % N]
            send(lines, lines, tzs.at[1, d], tzr.at[1, d], left)

    def a_table(i, block, device):
        send(ctab.at[block], ctab.at[block], tcs.at[i], tcr.at[i], device)

    def a_table_received(i, block):
        received(ctab.at[block], tcr.at[i], tcs.at[i])

    def a_send(i, block, part, device):
        ref = abuf.at[block, pl.ds(0, CAP_A)] if part is None else abuf.at[block, pl.ds(0, CAP_A), pl.ds(part * H, H)]
        send(ref, ref, as_.at[i], ar.at[i], device)

    def a_received(i, block, part):
        ref = abuf.at[block, pl.ds(0, CAP_A)] if part is None else abuf.at[block, pl.ds(0, CAP_A), pl.ds(part * H, H)]
        received(ref, ar.at[i], as_.at[i])

    def a_first(base, block):
        a_send(base, block, None, xright)
        a_send(base + 1, block, None, xleft)
        a_table(base, block, xright)
        a_table(base + 1, block, xleft)

    def a_forward(base, block):
        a_received(base, (block + N - 2) % N, None)
        a_send(base + 2, (block + N - 2) % N, 0, xright)
        a_table_received(base, (block + N - 2) % N)
        a_table(base + 2, (block + N - 2) % N, xright)
        a_received(base + 1, (block + 2) % N, None)
        a_send(base + 3, (block + 2) % N, 1, xleft)
        a_table_received(base + 1, (block + 2) % N)

    def a_last(base, block):
        a_received(base + 2, (block + 4) % N, 0)
        a_received(base + 3, (block + 4) % N, 1)
        a_table_received(base + 2, (block + 4) % N)

    started = [0, 1]
    z_send(0)
    z_send(1)
    for ref in (own, l1, l2, l3, r1, r2, r3, x4):
        ref[0][CAP_B] = jnp.zeros((T, H), jnp.bfloat16)
        for p in (1, 2):
            ref[p][CAP_B] = jnp.zeros((Q, T), jnp.bfloat16)
    for c in range(N):
        abuf[c, CAP_A] = jnp.zeros((T, T), jnp.bfloat16)

    low = lax.broadcasted_iota(jnp.int32, (H, H), 1) < Q
    lane = lax.broadcasted_iota(jnp.int32, (8, 128), 1)
    table = jnp.where(lane < LANE_A, CAP_B, CAP_A)
    for s in range(CAP_B):
        table = jnp.where(lane == rs[s], s, table)
    for s in range(CAP_A):
        table = jnp.where(lane == ls[s] + LANE_A, s, table)
    ztab[row] = table
    ctab[col] = table
    local[0].wait()
    a_send(8, col, None, ypair)
    a_table(8, col, ypair)
    a_first(0, col)
    z_table(1)
    acc[...] = jnp.zeros_like(acc)
    lanes[...] = jnp.zeros_like(lanes)
    local[1].wait()
    local[2].wait()
    for tile in range(CAP_B):
        turned = raw[tile].T
        own1[tile] = turned[:Q]
        own2[tile] = turned[Q:]

    def tables():
        received(ztab.at[(row + 4) % N], tzr.at[0, 4], tzs.at[0, 4])
        c1 = pltpu.make_async_copy(ztab, zsm, loc.at[3])
        c2 = pltpu.make_async_copy(ctab, csm, loc.at[4])
        c1.start()
        c2.start()
        c1.wait()
        c2.wait()

    def densify_a(first, last):
        def body(c, carry):
            for i in range(ROW_T):
                for kk in range(KT):
                    s = csm[c, 0, LANE_A + i * KT + kk]
                    adense[c, pl.ds(i * T, T), pl.ds(kk * T, T)] = abuf[c, s]
            return carry

        lax.fori_loop(first, last, body, 0)

    def compute(p, ref, j, after=None):
        for kk in range(KT):
            for jc in range(COL_T):
                s = zsm[j, 0, kk * COL_T + jc]
                if p == 0:
                    bdense[jc // 2, pl.ds(kk * T, T), pl.ds((jc % 2) * H, H)] = ref[p][s]
                else:
                    bturned[pl.ds(jc * Q, Q), pl.ds(kk * T, T)] = ref[p][s]
        for n in range(2) if p == 0 else (p + 1,):
            for i in range(ROW_T):
                rows = adense[j, pl.ds(i * T, T)]
                if p == 0:
                    part = jnp.dot(rows, bdense[n], preferred_element_type=jnp.float32)
                else:
                    part = lax.dot_general(
                        rows, bturned[...], (((1,), (1,)), ((), ())), preferred_element_type=jnp.float32
                    )
                acc[n, 0, i] += part[:H]
                acc[n, 1, i] += part[H:]
            if after is not None:
                after(n)

    def layer_send(n):
        send(acc.at[n, 1 - core], in1.at[n], s1s.at[n], s1r.at[n], core_peer)

    def layer_forward(n):
        received(in1.at[n], s1r.at[n], s1s.at[n])
        acc[n, core, 1 - ylo] += in1[n, 1 - ylo]
        send(acc.at[n, core, 1 - ylo], in2.at[n], s2s.at[n], s2r.at[n], y_peer)

    def layer_finish(n):
        received(in2.at[n], s2r.at[n], s2s.at[n])
        finish(n, acc[n, core, ylo] + in1[n, ylo] + in2[n])

    def finish(n, total):
        squares = total * total
        lanes[...] += squares[:, :H] + squares[:, H:]
        for u in range(2):
            part = squares[:, u * H : (u + 1) * H]
            if n < 2:
                out[:, pl.ds((n * 2 + u) * T, H)] = part
                continue
            turned = pltpu.roll(part, Q, 1)
            for v in range(2):
                place = pl.ds((u * 2 + v) * T + H, H)
                if n == 2:
                    out[:, place] = turned if v else part
                else:
                    out[:, place] = jnp.where(low, out[:, place], part if v else turned)

    def code(v):
        steps = (jnp.log2(jnp.maximum(v, 2.0**LOWEST)) - LOWEST) * STEPS
        steps = jnp.minimum(jnp.round(steps), 65534.0) - 32767.0
        return jnp.where(v > 0, steps, float(ZERO)).astype(jnp.int32).astype(jnp.int16)

    def decode(q):
        steps = q.astype(jnp.int32).astype(jnp.float32)
        v = jnp.exp2((steps + 32767.0) * (1.0 / STEPS) + LOWEST)
        return jnp.where(steps > ZERO + 0.5, v, 0.0)

    def across(c):
        return {"layer": (1 - ylo) * 2 + c}

    def last_send():
        send(acc.at[3, 1 - core, ylo], in1.at[3, 0], s1s.at[3], s1r.at[3], core_peer)
        for u in range(2):
            c = core if u else 1 - core
            coded[u] = code(acc[3, c, 1 - ylo])
            send(coded.at[u], incoded.at[core], s2s.at[3 + u], s2r.at[3 + u], across(c))

    def last_finish():
        received(in1.at[3, 0], s1r.at[3], s1s.at[3])
        total = acc[3, core, ylo] + in1[3, 0]
        for u in range(2):
            c = core if u else 1 - core
            received(incoded.at[c], s2r.at[3 + u], s2s.at[3 + u])
            total += decode(incoded[c])
        finish(3, total)

    def at_left(d):
        return (row + N - d) % N

    def at_right(d):
        return (row + d) % N

    last = len(ORDER) - 1
    for k in range(last):
        z_step(k)
        if k >= 3:
            sent(len(pending) - SENT_LATER)
        if k == 0:
            z_table(2)
        elif k == 1:
            z_table(3)
        elif k == 2:
            z_table(4)
            a_forward(0, col)
            a_received(8, ypair_col, None)
            a_table_received(8, ypair_col)
            a_first(4, ypair_col)
        elif k == 4:
            a_last(0, col)
        elif k == 5:
            a_forward(4, ypair_col)
        elif k == 8:
            a_last(4, ypair_col)
            tables()
            densify_a(0, N // 2)
        elif k == 9:
            densify_a(N // 2, N)
        elif k == 10:
            compute(0, own, row)
            compute(0, l1, at_left(1))
        elif k == 11:
            compute(0, r1, at_right(1))
            compute(0, l2, at_left(2))
        elif k == 12:
            compute(0, r2, at_right(2))
            compute(0, l3, at_left(3))
        elif k == 13:
            compute(0, r3, at_right(3))
            compute(0, x4, at_left(4), layer_send)
        elif k == 14:
            compute(1, own, row)
            compute(1, l1, at_left(1))
            compute(1, r1, at_right(1))
            layer_forward(0)
            layer_forward(1)
        elif k == 15:
            compute(1, l2, at_left(2))
            compute(1, r2, at_right(2))
            compute(1, l3, at_left(3))
            compute(1, r3, at_right(3))
        elif k == 16:
            compute(1, x4, at_left(4), layer_send)
            compute(2, own, row)
            compute(2, l1, at_left(1))
            compute(2, r1, at_right(1))
        elif k == 17:
            layer_forward(2)
            layer_finish(0)
        elif k == 18:
            layer_finish(1)
            compute(2, l2, at_left(2))
            compute(2, r2, at_right(2))
        elif k == 19:
            compute(2, l3, at_left(3))
            compute(2, r3, at_right(3))
    z_step(last)
    compute(2, x4, at_left(4))
    last_send()
    layer_finish(2)
    last_finish()

    line = jnp.sum(lanes[...].T, axis=0, keepdims=True)
    line = jnp.broadcast_to(line, (8, 128))
    mytot[...] = line
    for o in range(1, N):
        send(mytot, ctot.at[col], tos.at[o], tor.at[o], {"col": (col + o) % N})
    ctot[col] = line
    sent(len(pending) - (N - 1))
    for o in range(1, N):
        received(ctot.at[(col + N - o) % N], tor.at[o], tos.at[o])
    total = ctot[0]
    for c in range(1, N):
        total += ctot[c]
    scale = jnp.broadcast_to((COLS / total)[0:1], (H, H)).T
    for u in range(8):
        out[:, pl.ds(u * H, H)] *= scale
    sent(len(pending))


def local(left_tiles, left_slots, right_tiles, right_slots):
    bf16, f32, i32 = jnp.bfloat16, jnp.float32, jnp.int32
    dma = pltpu.SemaphoreType.DMA
    block = pltpu.VMEM((CAP_B + 1, T, H), bf16)
    turned = pltpu.VMEM((CAP_B + 1, Q, T), bf16)
    return pl.pallas_call(
        kernel,
        out_shape=jax.ShapeDtypeStruct((H, 1024), f32),
        in_specs=[
            pl.BlockSpec(memory_space=pl.ANY),
            pl.BlockSpec(memory_space=pltpu.SMEM),
            pl.BlockSpec(memory_space=pl.ANY),
            pl.BlockSpec(memory_space=pltpu.SMEM),
        ],
        out_specs=pl.BlockSpec(memory_space=pltpu.VMEM),
        scratch_shapes=[
            *[block] * 8,
            *[turned] * 16,
            pltpu.VMEM((CAP_B, T, H), bf16),
            pltpu.VMEM((N, CAP_A + 1, T, T), bf16),
            pltpu.VMEM((N, ROW_T * T, KT * T), bf16),
            pltpu.VMEM((2, KT * T, T), bf16),
            pltpu.VMEM((4 * Q, KT * T), bf16),
            pltpu.VMEM((4, 2, 2, H, T), f32),
            pltpu.VMEM((4, 2, H, T), f32),
            pltpu.VMEM((4, H, T), f32),
            pltpu.VMEM((2, H, T), jnp.int16),
            pltpu.VMEM((2, H, T), jnp.int16),
            pltpu.VMEM((H, H), f32),
            pltpu.VMEM((N, 8, 128), i32),
            pltpu.VMEM((N, 8, 128), i32),
            pltpu.SMEM((N, 8, 128), i32),
            pltpu.SMEM((N, 8, 128), i32),
            pltpu.VMEM((8, 128), f32),
            pltpu.VMEM((N, 8, 128), f32),
            dma((2, len(ORDER))), dma((2, len(ORDER))),
            dma((9,)), dma((9,)),
            dma((2, 5)), dma((2, 5)), dma((9,)), dma((9,)), dma((N,)), dma((N,)),
            dma((4,)), dma((4,)), dma((5,)), dma((5,)),
            dma((5,)),
        ],
        compiler_params=pltpu.CompilerParams(
            collective_id=0, has_side_effects=True, vmem_limit_bytes=56 * 1024 * 1024
        ),
        cost_estimate=pl.CostEstimate(flops=8_600_000_000, bytes_accessed=2_000_000, transcendentals=0),
    )(
        left_tiles.reshape(CAP_A, T, T),
        left_slots.reshape(CAP_A),
        right_tiles.reshape(CAP_B, T, T),
        right_slots.reshape(CAP_B),
    )


def solution(mesh):
    return jax.shard_map(
        local,
        mesh=mesh,
        in_specs=(
            P("row", "layer", "col", None, None, None),
            P("row", "layer", "col", None),
            P("row", "layer", "col", None, None, None),
            P("row", "layer", "col", None),
        ),
        out_specs=P(("row", "layer"), "col"),
        check_vma=False,
    )
```

```python
import jax
import jax.numpy as jnp
from jax import lax
from jax.experimental import pallas as pl
from jax.experimental.pallas import tpu as pltpu
from jax.sharding import PartitionSpec as P

MESH = pl.DeviceIdType.MESH
T = 256
H = 128
N = 8
CAP_A, CAP_B = 3, 6
KT = 4
COL_T = 4
Q = 64
ROW_T = 2
COLS = 8192
SENT_LATER = 24
LANE_A = 64
HALF = CAP_B // 2
LOWEST, STEPS, ZERO = -6.0, 65534 / 23, -32768
ORDER = [(0, 1, 0), (0, 1, 1), (0, 2, 0), (0, 2, 1), (0, 3, 0), (0, 3, 1), (0, 4, 0)]
ORDER += [(1, 1, 0), (1, 1, 1), (2, 1, 0), (1, 2, 0), (1, 2, 1), (2, 1, 1), (1, 3, 0), (1, 3, 1)]
ORDER += [(2, 2, 0), (1, 4, 0), (2, 2, 1), (2, 3, 0), (2, 3, 1), (2, 4, 0)]


def kernel(
    lt, ls, rt, rs, out,
    own0, l10, l20, l30, r10, r20, r30, x40,
    own1, l11, l21, l31, r11, r21, r31, x41,
    own2, l12, l22, l32, r12, r22, r32, x42,
    raw,
    abuf, adense, bdense, bturned, acc, in1, in2, coded, incoded, lanes,
    ztab, ctab, zsm, csm, mytot, ctot,
    zs, zr, as_, ar, tzs, tzr, tcs, tcr, tos, tor, s1s, s1r, s2s, s2r, loc,
):
    row = lax.axis_index("row")
    col = lax.axis_index("col")
    layer = lax.axis_index("layer")
    core, ylo = layer % 2, layer // 2
    pending = []
    own, x4 = (own0, own1, own2), (x40, x41, x42)
    l1, l2, l3 = (l10, l11, l12), (l20, l21, l22), (l30, l31, l32)
    r1, r2, r3 = (r10, r11, r12), (r20, r21, r22), (r30, r31, r32)

    def send(src, dst, ss, rs_, device):
        copy = pltpu.make_async_remote_copy(
            src_ref=src, dst_ref=dst, send_sem=ss, recv_sem=rs_, device_id=device, device_id_type=MESH
        )
        copy.start()
        pending.append(copy)

    def sent(count):
        for copy in pending[: max(count, 0)]:
            copy.wait_send()
        del pending[: max(count, 0)]

    def received(dst, rs_, ss):
        pltpu.make_async_remote_copy(
            src_ref=dst, dst_ref=dst, send_sem=ss, recv_sem=rs_, device_id={"row": (row + 1) % N}, device_id_type=MESH
        ).wait_recv()

    core_peer = {"layer": ylo * 2 + (1 - core)}
    y_peer = {"layer": (1 - ylo) * 2 + core}
    right, left = {"row": (row + 1) % N}, {"row": (row + N - 1) % N}
    xright, xleft = {"col": (col + 2) % N}, {"col": (col + N - 2) % N}
    ypair_col = col + 1 - 2 * (col % 2)
    ypair = {"col": ypair_col}
    peers = [right, left, xright, xleft, ypair, core_peer, y_peer]
    barrier = pltpu.get_barrier_semaphore()
    for peer in peers:
        pl.semaphore_signal(barrier, inc=1, device_id=peer, device_id_type=MESH)

    local = [pltpu.make_async_copy(lt, abuf.at[col, pl.ds(0, CAP_A)], loc.at[0])]
    local.append(pltpu.make_async_copy(rt.at[:, :, pl.ds(0, H)], own0.at[pl.ds(0, CAP_B)], loc.at[1]))
    local.append(pltpu.make_async_copy(rt.at[:, :, pl.ds(H, H)], raw, loc.at[2]))
    for copy in local:
        copy.start()
    pl.semaphore_wait(barrier, len(peers))

    from_left = [None, l1, l2, l3, x4]
    from_right = [None, r1, r2, r3, x4]

    def z_send(k):
        p, d, q = ORDER[k]
        for way, (held, device) in enumerate(((from_left, right), (from_right, left))):
            piece = pl.ds((q if way == 0 else 1 - q) * HALF, HALF)
            if d > 1:
                src = held[d - 1][p].at[piece]
            elif p == 0:
                src = rt.at[piece, :, pl.ds(0, H)]
            else:
                src = own[p].at[piece]
            send(src, held[d][p].at[piece], zs.at[way, k], zr.at[way, k], device)

    def z_step(k):
        p, d, q = ORDER[k]
        for way, held in enumerate((from_left, from_right)):
            piece = pl.ds((q if way == 0 else 1 - q) * HALF, HALF)
            received(held[d][p].at[piece], zr.at[way, k], zs.at[way, k])
        while len(started) < len(ORDER):
            j = len(started)
            p, d, q = ORDER[j]
            if j - k > (2 if p == 0 else 4) or (d > 1 and ORDER.index((p, d - 1, q)) > k):
                break
            started.append(j)
            z_send(j)

    def z_table(d):
        if d > 1:
            received(ztab.at[(row + N - d + 1) % N], tzr.at[0, d - 1], tzs.at[0, d - 1])
            received(ztab.at[(row + d - 1) % N], tzr.at[1, d - 1], tzs.at[1, d - 1])
        lines = ztab.at[(row + N - d + 1) % N]
        send(lines, lines, tzs.at[0, d], tzr.at[0, d], right)
        if d < 4:
            lines = ztab.at[(row + d - 1) % N]
            send(lines, lines, tzs.at[1, d], tzr.at[1, d], left)

    def a_table(i, block, device):
        send(ctab.at[block], ctab.at[block], tcs.at[i], tcr.at[i], device)

    def a_table_received(i, block):
        received(ctab.at[block], tcr.at[i], tcs.at[i])

    def a_send(i, block, part, device):
        ref = abuf.at[block, pl.ds(0, CAP_A)] if part is None else abuf.at[block, pl.ds(0, CAP_A), pl.ds(part * H, H)]
        send(ref, ref, as_.at[i], ar.at[i], device)

    def a_received(i, block, part):
        ref = abuf.at[block, pl.ds(0, CAP_A)] if part is None else abuf.at[block, pl.ds(0, CAP_A), pl.ds(part * H, H)]
        received(ref, ar.at[i], as_.at[i])

    def a_first(base, block):
        a_send(base, block, None, xright)
        a_send(base + 1, block, None, xleft)
        a_table(base, block, xright)
        a_table(base + 1, block, xleft)

    def a_forward(base, block):
        a_received(base, (block + N - 2) % N, None)
        a_send(base + 2, (block + N - 2) % N, 0, xright)
        a_table_received(base, (block + N - 2) % N)
        a_table(base + 2, (block + N - 2) % N, xright)
        a_received(base + 1, (block + 2) % N, None)
        a_send(base + 3, (block + 2) % N, 1, xleft)
        a_table_received(base + 1, (block + 2) % N)

    def a_last(base, block):
        a_received(base + 2, (block + 4) % N, 0)
        a_received(base + 3, (block + 4) % N, 1)
        a_table_received(base + 2, (block + 4) % N)

    started = [0, 1]
    z_send(0)
    z_send(1)
    for ref in (own, l1, l2, l3, r1, r2, r3, x4):
        ref[0][CAP_B] = jnp.zeros((T, H), jnp.bfloat16)
        for p in (1, 2):
            ref[p][CAP_B] = jnp.zeros((Q, T), jnp.bfloat16)
    for c in range(N):
        abuf[c, CAP_A] = jnp.zeros((T, T), jnp.bfloat16)

    low = lax.broadcasted_iota(jnp.int32, (H, H), 1) < Q
    lane = lax.broadcasted_iota(jnp.int32, (8, 128), 1)
    table = jnp.where(lane < LANE_A, CAP_B, CAP_A)
    for s in range(CAP_B):
        table = jnp.where(lane == rs[s], s, table)
    for s in range(CAP_A):
        table = jnp.where(lane == ls[s] + LANE_A, s, table)
    ztab[row] = table
    ctab[col] = table
    local[0].wait()
    a_send(8, col, None, ypair)
    a_table(8, col, ypair)
    a_first(0, col)
    z_table(1)
    acc[...] = jnp.zeros_like(acc)
    lanes[...] = jnp.zeros_like(lanes)
    local[1].wait()
    local[2].wait()
    for tile in range(CAP_B):
        turned = raw[tile].T
        own1[tile] = turned[:Q]
        own2[tile] = turned[Q:]

    def tables():
        received(ztab.at[(row + 4) % N], tzr.at[0, 4], tzs.at[0, 4])
        c1 = pltpu.make_async_copy(ztab, zsm, loc.at[3])
        c2 = pltpu.make_async_copy(ctab, csm, loc.at[4])
        c1.start()
        c2.start()
        c1.wait()
        c2.wait()

    def densify_a(first, last):
        def body(c, carry):
            for i in range(ROW_T):
                for kk in range(KT):
                    s = csm[c, 0, LANE_A + i * KT + kk]
                    adense[c, pl.ds(i * T, T), pl.ds(kk * T, T)] = abuf[c, s]
            return carry

        lax.fori_loop(first, last, body, 0)

    def compute(p, ref, j, after=None):
        for kk in range(KT):
            for jc in range(COL_T):
                s = zsm[j, 0, kk * COL_T + jc]
                if p == 0:
                    bdense[jc // 2, pl.ds(kk * T, T), pl.ds((jc % 2) * H, H)] = ref[p][s]
                else:
                    bturned[pl.ds(jc * Q, Q), pl.ds(kk * T, T)] = ref[p][s]
        for n in range(2) if p == 0 else (p + 1,):
            for i in range(ROW_T):
                rows = adense[j, pl.ds(i * T, T)]
                if p == 0:
                    part = jnp.dot(rows, bdense[n], preferred_element_type=jnp.float32)
                else:
                    part = lax.dot_general(
                        rows, bturned[...], (((1,), (1,)), ((), ())), preferred_element_type=jnp.float32
                    )
                acc[n, 0, i] += part[:H]
                acc[n, 1, i] += part[H:]
            if after is not None:
                after(n)

    def layer_send(n):
        send(acc.at[n, 1 - core], in1.at[n], s1s.at[n], s1r.at[n], core_peer)

    def layer_forward(n):
        received(in1.at[n], s1r.at[n], s1s.at[n])
        acc[n, core, 1 - ylo] += in1[n, 1 - ylo]
        send(acc.at[n, core, 1 - ylo], in2.at[n], s2s.at[n], s2r.at[n], y_peer)

    def layer_finish(n):
        received(in2.at[n], s2r.at[n], s2s.at[n])
        finish(n, acc[n, core, ylo] + in1[n, ylo] + in2[n])

    def finish(n, total):
        squares = total * total
        lanes[...] += squares[:, :H] + squares[:, H:]
        for u in range(2):
            part = squares[:, u * H : (u + 1) * H]
            if n < 2:
                out[:, pl.ds((n * 2 + u) * T, H)] = part
                continue
            turned = pltpu.roll(part, Q, 1)
            for v in range(2):
                place = pl.ds((u * 2 + v) * T + H, H)
                if n == 2:
                    out[:, place] = turned if v else part
                else:
                    out[:, place] = jnp.where(low, out[:, place], part if v else turned)

    def code(v):
        steps = (jnp.log2(jnp.maximum(v, 2.0**LOWEST)) - LOWEST) * STEPS
        steps = jnp.minimum(jnp.round(steps), 65534.0) - 32767.0
        return jnp.where(v > 0, steps, float(ZERO)).astype(jnp.int32).astype(jnp.int16)

    def decode(q):
        steps = q.astype(jnp.int32).astype(jnp.float32)
        v = jnp.exp2((steps + 32767.0) * (1.0 / STEPS) + LOWEST)
        return jnp.where(steps > ZERO + 0.5, v, 0.0)

    def across(c):
        return {"layer": (1 - ylo) * 2 + c}

    def last_send():
        send(acc.at[3, 1 - core, ylo], in1.at[3, 0], s1s.at[3], s1r.at[3], core_peer)
        for u in range(2):
            c = core if u else 1 - core
            coded[u] = code(acc[3, c, 1 - ylo])
            send(coded.at[u], incoded.at[core], s2s.at[3 + u], s2r.at[3 + u], across(c))

    def last_finish():
        received(in1.at[3, 0], s1r.at[3], s1s.at[3])
        total = acc[3, core, ylo] + in1[3, 0]
        for u in range(2):
            c = core if u else 1 - core
            received(incoded.at[c], s2r.at[3 + u], s2s.at[3 + u])
            total += decode(incoded[c])
        finish(3, total)

    def at_left(d):
        return (row + N - d) % N

    def at_right(d):
        return (row + d) % N

    last = len(ORDER) - 1
    for k in range(last):
        z_step(k)
        if k >= 3:
            sent(len(pending) - SENT_LATER)
        if k == 0:
            z_table(2)
        elif k == 1:
            z_table(3)
        elif k == 2:
            z_table(4)
            a_forward(0, col)
            a_received(8, ypair_col, None)
            a_table_received(8, ypair_col)
            a_first(4, ypair_col)
        elif k == 4:
            a_last(0, col)
        elif k == 5:
            a_forward(4, ypair_col)
        elif k == 8:
            a_last(4, ypair_col)
            tables()
            densify_a(0, N // 2)
        elif k == 9:
            densify_a(N // 2, N)
        elif k == 10:
            compute(0, own, row)
            compute(0, l1, at_left(1))
        elif k == 11:
            compute(0, r1, at_right(1))
            compute(0, l2, at_left(2))
        elif k == 12:
            compute(0, r2, at_right(2))
            compute(0, l3, at_left(3))
        elif k == 13:
            compute(0, r3, at_right(3))
            compute(0, x4, at_left(4), layer_send)
        elif k == 14:
            compute(1, own, row)
            compute(1, l1, at_left(1))
            compute(1, r1, at_right(1))
            layer_forward(0)
            layer_forward(1)
        elif k == 15:
            compute(1, l2, at_left(2))
            compute(1, r2, at_right(2))
            compute(1, l3, at_left(3))
            compute(1, r3, at_right(3))
        elif k == 16:
            compute(1, x4, at_left(4), layer_send)
            compute(2, own, row)
            compute(2, l1, at_left(1))
            compute(2, r1, at_right(1))
        elif k == 17:
            layer_forward(2)
            layer_finish(0)
        elif k == 18:
            layer_finish(1)
            compute(2, l2, at_left(2))
            compute(2, r2, at_right(2))
        elif k == 19:
            compute(2, l3, at_left(3))
            compute(2, r3, at_right(3))
    z_step(last)
    compute(2, x4, at_left(4))
    last_send()
    layer_finish(2)
    last_finish()

    line = jnp.sum(lanes[...].T, axis=0, keepdims=True)
    line = jnp.broadcast_to(line, (8, 128))
    mytot[...] = line
    for o in range(1, N):
        send(mytot, ctot.at[col], tos.at[o], tor.at[o], {"col": (col + o) % N})
    ctot[col] = line
    sent(len(pending) - (N - 1))
    for o in range(1, N):
        received(ctot.at[(col + N - o) % N], tor.at[o], tos.at[o])
    total = ctot[0]
    for c in range(1, N):
        total += ctot[c]
    scale = jnp.broadcast_to((COLS / total)[0:1], (H, H)).T
    for u in range(8):
        out[:, pl.ds(u * H, H)] *= scale
    sent(len(pending))


def local(left_tiles, left_slots, right_tiles, right_slots):
    bf16, f32, i32 = jnp.bfloat16, jnp.float32, jnp.int32
    dma = pltpu.SemaphoreType.DMA
    block = pltpu.VMEM((CAP_B + 1, T, H), bf16)
    turned = pltpu.VMEM((CAP_B + 1, Q, T), bf16)
    return pl.pallas_call(
        kernel,
        out_shape=pltpu.VMEM((H, 1024), f32),
        in_specs=[
            pl.BlockSpec(memory_space=pl.ANY),
            pl.BlockSpec(memory_space=pltpu.SMEM),
            pl.BlockSpec(memory_space=pl.ANY),
            pl.BlockSpec(memory_space=pltpu.SMEM),
        ],
        out_specs=pl.BlockSpec(memory_space=pltpu.VMEM),
        scratch_shapes=[
            *[block] * 8,
            *[turned] * 16,
            pltpu.VMEM((CAP_B, T, H), bf16),
            pltpu.VMEM((N, CAP_A + 1, T, T), bf16),
            pltpu.VMEM((N, ROW_T * T, KT * T), bf16),
            pltpu.VMEM((2, KT * T, T), bf16),
            pltpu.VMEM((4 * Q, KT * T), bf16),
            pltpu.VMEM((4, 2, 2, H, T), f32),
            pltpu.VMEM((4, 2, H, T), f32),
            pltpu.VMEM((4, H, T), f32),
            pltpu.VMEM((2, H, T), jnp.int16),
            pltpu.VMEM((2, H, T), jnp.int16),
            pltpu.VMEM((H, H), f32),
            pltpu.VMEM((N, 8, 128), i32),
            pltpu.VMEM((N, 8, 128), i32),
            pltpu.SMEM((N, 8, 128), i32),
            pltpu.SMEM((N, 8, 128), i32),
            pltpu.VMEM((8, 128), f32),
            pltpu.VMEM((N, 8, 128), f32),
            dma((2, len(ORDER))), dma((2, len(ORDER))),
            dma((9,)), dma((9,)),
            dma((2, 5)), dma((2, 5)), dma((9,)), dma((9,)), dma((N,)), dma((N,)),
            dma((4,)), dma((4,)), dma((5,)), dma((5,)),
            dma((5,)),
        ],
        compiler_params=pltpu.CompilerParams(
            collective_id=0, has_side_effects=True, vmem_limit_bytes=54 * 1024 * 1024
        ),
        cost_estimate=pl.CostEstimate(flops=8_600_000_000, bytes_accessed=2_000_000, transcendentals=0),
    )(
        left_tiles.reshape(CAP_A, T, T),
        left_slots.reshape(CAP_A),
        right_tiles.reshape(CAP_B, T, T),
        right_slots.reshape(CAP_B),
    )


def solution(mesh):
    return jax.shard_map(
        local,
        mesh=mesh,
        in_specs=(
            P("row", "layer", "col", None, None, None),
            P("row", "layer", "col", None),
            P("row", "layer", "col", None, None, None),
            P("row", "layer", "col", None),
        ),
        out_specs=P(("row", "layer"), "col"),
        check_vma=False,
    )
```

```python
import jax
import jax.numpy as jnp
from jax import lax
from jax.experimental import pallas as pl
from jax.experimental.pallas import tpu as pltpu
from jax.sharding import PartitionSpec as P

MESH = pl.DeviceIdType.MESH
T = 256
H = 128
N = 8
CAP_A, CAP_B = 3, 6
KT = 4
COL_T = 4
Q = 64
ROW_T = 2
COLS = 8192
WAYS = (0, 1)
SENT_LATER = 24
LANE_A = 64
HALF = CAP_B // 2
LOWEST, STEPS, ZERO = -6.0, 65534 / 23, -32768
ORDER = [(0, 1, 0), (0, 1, 1), (0, 2, 0), (0, 2, 1), (0, 3, 0), (0, 3, 1), (0, 4, 0)]
ORDER += [(1, 1, 0), (1, 1, 1), (2, 1, 0), (1, 2, 0), (1, 2, 1), (2, 1, 1), (1, 3, 0), (1, 3, 1)]
ORDER += [(2, 2, 0), (1, 4, 0), (2, 2, 1), (2, 3, 0), (2, 3, 1), (2, 4, 0)]


def kernel(
    lt, left_slots, rt, right_slots, out,
    own0, l10, l20, l30, r10, r20, r30, x40,
    own1, l11, l21, l31, r11, r21, r31, x41,
    own2, l12, l22, l32, r12, r22, r32, x42,
    raw,
    abuf, adense, bdense, bturned, acc, in1, in2, coded, incoded, lanes,
    ztab, ctab, zsm, csm, mytot, ctot,
    zs, zr, as_, ar, tzs, tzr, tcs, tcr, tos, tor, s1s, s1r, s2s, s2r, loc, ls, rs,
):
    row = lax.axis_index("row")
    col = lax.axis_index("col")
    layer = lax.axis_index("layer")
    core, ylo = layer % 2, layer // 2
    pending = []
    own, x4 = (own0, own1, own2), (x40, x41, x42)
    l1, l2, l3 = (l10, l11, l12), (l20, l21, l22), (l30, l31, l32)
    r1, r2, r3 = (r10, r11, r12), (r20, r21, r22), (r30, r31, r32)

    def send(src, dst, ss, rs_, device):
        copy = pltpu.make_async_remote_copy(
            src_ref=src, dst_ref=dst, send_sem=ss, recv_sem=rs_, device_id=device, device_id_type=MESH
        )
        copy.start()
        pending.append(copy)

    def sent(count):
        for copy in pending[: max(count, 0)]:
            copy.wait_send()
        del pending[: max(count, 0)]

    def received(dst, rs_, ss):
        pltpu.make_async_remote_copy(
            src_ref=dst, dst_ref=dst, send_sem=ss, recv_sem=rs_, device_id={"row": (row + 1) % N}, device_id_type=MESH
        ).wait_recv()

    core_peer = {"layer": ylo * 2 + (1 - core)}
    y_peer = {"layer": (1 - ylo) * 2 + core}
    right, left = {"row": (row + 1) % N}, {"row": (row + N - 1) % N}
    xright, xleft = {"col": (col + 2) % N}, {"col": (col + N - 2) % N}
    ypair_col = col + 1 - 2 * (col % 2)
    ypair = {"col": ypair_col}
    peers = [right, left, xright, xleft, ypair, core_peer, y_peer]
    barrier = pltpu.get_barrier_semaphore()
    for peer in peers:
        pl.semaphore_signal(barrier, inc=1, device_id=peer, device_id_type=MESH)

    local = [pltpu.make_async_copy(lt, abuf.at[col, pl.ds(0, CAP_A)], loc.at[0])]
    local.append(pltpu.make_async_copy(rt.at[:, :, pl.ds(0, H)], own0.at[pl.ds(0, CAP_B)], loc.at[1]))
    local.append(pltpu.make_async_copy(rt.at[:, :, pl.ds(H, H)], raw, loc.at[2]))
    local.append(pltpu.make_async_copy(left_slots, ls, loc.at[5]))
    local.append(pltpu.make_async_copy(right_slots, rs, loc.at[6]))
    for copy in local:
        copy.start()
    pl.semaphore_wait(barrier, len(peers))

    from_left = [None, l1, l2, l3, x4]
    from_right = [None, r1, r2, r3, x4]

    def z_send(k, way):
        held, device = ((from_left, right), (from_right, left))[way]
        p, d, q = ORDER[k]
        piece = pl.ds((q if way == 0 else 1 - q) * HALF, HALF)
        if d > 1:
            src = held[d - 1][p].at[piece]
        elif p == 0:
            src = rt.at[piece, :, pl.ds(0, H)]
        else:
            src = own[p].at[piece]
        send(src, held[d][p].at[piece], zs.at[way, k], zr.at[way, k], device)

    def z_step(k):
        for way in WAYS:
            p, d, q = ORDER[k]
            piece = pl.ds((q if way == 0 else 1 - q) * HALF, HALF)
            received((from_left, from_right)[way][d][p].at[piece], zr.at[way, k], zs.at[way, k])
            while started[way] < len(ORDER):
                j = started[way]
                p, d, q = ORDER[j]
                if j - k > (2 if p == 0 else 4) or (d > 1 and ORDER.index((p, d - 1, q)) > k):
                    break
                started[way] += 1
                z_send(j, way)

    def z_table(d):
        if d > 1:
            received(ztab.at[(row + N - d + 1) % N], tzr.at[0, d - 1], tzs.at[0, d - 1])
            received(ztab.at[(row + d - 1) % N], tzr.at[1, d - 1], tzs.at[1, d - 1])
        lines = ztab.at[(row + N - d + 1) % N]
        send(lines, lines, tzs.at[0, d], tzr.at[0, d], right)
        if d < 4:
            lines = ztab.at[(row + d - 1) % N]
            send(lines, lines, tzs.at[1, d], tzr.at[1, d], left)

    def a_table(i, block, device):
        send(ctab.at[block], ctab.at[block], tcs.at[i], tcr.at[i], device)

    def a_table_received(i, block):
        received(ctab.at[block], tcr.at[i], tcs.at[i])

    def a_send(i, block, part, device):
        ref = abuf.at[block, pl.ds(0, CAP_A)] if part is None else abuf.at[block, pl.ds(0, CAP_A), pl.ds(part * H, H)]
        send(ref, ref, as_.at[i], ar.at[i], device)

    def a_received(i, block, part):
        ref = abuf.at[block, pl.ds(0, CAP_A)] if part is None else abuf.at[block, pl.ds(0, CAP_A), pl.ds(part * H, H)]
        received(ref, ar.at[i], as_.at[i])

    def a_first(base, block):
        a_send(base, block, None, xright)
        a_send(base + 1, block, None, xleft)
        a_table(base, block, xright)
        a_table(base + 1, block, xleft)

    def a_forward(base, block):
        a_received(base, (block + N - 2) % N, None)
        a_send(base + 2, (block + N - 2) % N, 0, xright)
        a_table_received(base, (block + N - 2) % N)
        a_table(base + 2, (block + N - 2) % N, xright)
        a_received(base + 1, (block + 2) % N, None)
        a_send(base + 3, (block + 2) % N, 1, xleft)
        a_table_received(base + 1, (block + 2) % N)

    def a_last(base, block):
        a_received(base + 2, (block + 4) % N, 0)
        a_received(base + 3, (block + 4) % N, 1)
        a_table_received(base + 2, (block + 4) % N)

    started = [2, 2]
    for way in WAYS:
        z_send(0, way)
        z_send(1, way)
    for ref in (own, l1, l2, l3, r1, r2, r3, x4):
        ref[0][CAP_B] = jnp.zeros((T, H), jnp.bfloat16)
        for p in (1, 2):
            ref[p][CAP_B] = jnp.zeros((Q, T), jnp.bfloat16)
    for c in range(N):
        abuf[c, CAP_A] = jnp.zeros((T, T), jnp.bfloat16)

    low = lax.broadcasted_iota(jnp.int32, (H, H), 1) < Q
    lane = lax.broadcasted_iota(jnp.int32, (8, 128), 1)
    table = jnp.where(lane < LANE_A, CAP_B, CAP_A)
    local[3].wait()
    local[4].wait()
    for s in range(CAP_B):
        table = jnp.where(lane == rs[s], s, table)
    for s in range(CAP_A):
        table = jnp.where(lane == ls[s] + LANE_A, s, table)
    ztab[row] = table
    ctab[col] = table
    local[0].wait()
    a_send(8, col, None, ypair)
    a_table(8, col, ypair)
    a_first(0, col)
    z_table(1)
    acc[...] = jnp.zeros_like(acc)
    lanes[...] = jnp.zeros_like(lanes)
    local[1].wait()
    local[2].wait()
    for tile in range(CAP_B):
        turned = raw[tile].T
        own1[tile] = turned[:Q]
        own2[tile] = turned[Q:]

    def tables():
        received(ztab.at[(row + 4) % N], tzr.at[0, 4], tzs.at[0, 4])
        c1 = pltpu.make_async_copy(ztab, zsm, loc.at[3])
        c2 = pltpu.make_async_copy(ctab, csm, loc.at[4])
        c1.start()
        c2.start()
        c1.wait()
        c2.wait()

    def densify_a(first, last):
        def body(c, carry):
            for i in range(ROW_T):
                for kk in range(KT):
                    s = csm[c, 0, LANE_A + i * KT + kk]
                    adense[c, pl.ds(i * T, T), pl.ds(kk * T, T)] = abuf[c, s]
            return carry

        lax.fori_loop(first, last, body, 0)

    def compute(p, ref, j, after=None):
        for kk in range(KT):
            for jc in range(COL_T):
                s = zsm[j, 0, kk * COL_T + jc]
                if p == 0:
                    bdense[jc // 2, pl.ds(kk * T, T), pl.ds((jc % 2) * H, H)] = ref[p][s]
                else:
                    bturned[pl.ds(jc * Q, Q), pl.ds(kk * T, T)] = ref[p][s]
        for n in range(2) if p == 0 else (p + 1,):
            for i in range(ROW_T):
                rows = adense[j, pl.ds(i * T, T)]
                if p == 0:
                    part = jnp.dot(rows, bdense[n], preferred_element_type=jnp.float32)
                else:
                    part = lax.dot_general(
                        rows, bturned[...], (((1,), (1,)), ((), ())), preferred_element_type=jnp.float32
                    )
                acc[n, 0, i] += part[:H]
                acc[n, 1, i] += part[H:]
            if after is not None:
                after(n)

    def layer_send(n):
        send(acc.at[n, 1 - core], in1.at[n], s1s.at[n], s1r.at[n], core_peer)

    def layer_forward(n):
        received(in1.at[n], s1r.at[n], s1s.at[n])
        acc[n, core, 1 - ylo] += in1[n, 1 - ylo]
        send(acc.at[n, core, 1 - ylo], in2.at[n], s2s.at[n], s2r.at[n], y_peer)

    def layer_finish(n):
        received(in2.at[n], s2r.at[n], s2s.at[n])
        finish(n, acc[n, core, ylo] + in1[n, ylo] + in2[n])

    def finish(n, total):
        squares = total * total
        lanes[...] += squares[:, :H] + squares[:, H:]
        for u in range(2):
            part = squares[:, u * H : (u + 1) * H]
            if n < 2:
                out[:, pl.ds((n * 2 + u) * T, H)] = part
                continue
            turned = pltpu.roll(part, Q, 1)
            for v in range(2):
                place = pl.ds((u * 2 + v) * T + H, H)
                if n == 2:
                    out[:, place] = turned if v else part
                else:
                    out[:, place] = jnp.where(low, out[:, place], part if v else turned)

    def code(v):
        steps = (jnp.log2(jnp.maximum(v, 2.0**LOWEST)) - LOWEST) * STEPS
        steps = jnp.minimum(jnp.round(steps), 65534.0) - 32767.0
        return jnp.where(v > 0, steps, float(ZERO)).astype(jnp.int32).astype(jnp.int16)

    def decode(q):
        steps = q.astype(jnp.int32).astype(jnp.float32)
        v = jnp.exp2((steps + 32767.0) * (1.0 / STEPS) + LOWEST)
        return jnp.where(steps > ZERO + 0.5, v, 0.0)

    def across(c):
        return {"layer": (1 - ylo) * 2 + c}

    def last_send():
        send(acc.at[3, 1 - core, ylo], in1.at[3, 0], s1s.at[3], s1r.at[3], core_peer)
        for u in range(2):
            c = core if u else 1 - core
            coded[u] = code(acc[3, c, 1 - ylo])
            send(coded.at[u], incoded.at[core], s2s.at[3 + u], s2r.at[3 + u], across(c))

    def last_finish():
        received(in1.at[3, 0], s1r.at[3], s1s.at[3])
        total = acc[3, core, ylo] + in1[3, 0]
        for u in range(2):
            c = core if u else 1 - core
            received(incoded.at[c], s2r.at[3 + u], s2s.at[3 + u])
            total += decode(incoded[c])
        finish(3, total)

    def at_left(d):
        return (row + N - d) % N

    def at_right(d):
        return (row + d) % N

    last = len(ORDER) - 1
    for k in range(last):
        z_step(k)
        if k >= 3:
            sent(len(pending) - SENT_LATER)
        if k == 0:
            z_table(2)
        elif k == 1:
            z_table(3)
        elif k == 2:
            z_table(4)
            a_forward(0, col)
            a_received(8, ypair_col, None)
            a_table_received(8, ypair_col)
            a_first(4, ypair_col)
        elif k == 4:
            a_last(0, col)
        elif k == 5:
            a_forward(4, ypair_col)
        elif k == 8:
            a_last(4, ypair_col)
            tables()
            densify_a(0, N // 2)
        elif k == 9:
            densify_a(N // 2, N)
        elif k == 10:
            compute(0, own, row)
            compute(0, l1, at_left(1))
        elif k == 11:
            compute(0, r1, at_right(1))
            compute(0, l2, at_left(2))
        elif k == 12:
            compute(0, r2, at_right(2))
            compute(0, l3, at_left(3))
        elif k == 13:
            compute(0, r3, at_right(3))
            compute(0, x4, at_left(4), layer_send)
        elif k == 14:
            compute(1, own, row)
            compute(1, l1, at_left(1))
            compute(1, r1, at_right(1))
            layer_forward(0)
            layer_forward(1)
        elif k == 15:
            compute(1, l2, at_left(2))
            compute(1, r2, at_right(2))
            compute(1, l3, at_left(3))
            compute(1, r3, at_right(3))
        elif k == 16:
            compute(1, x4, at_left(4), layer_send)
            compute(2, own, row)
            compute(2, l1, at_left(1))
            compute(2, r1, at_right(1))
        elif k == 17:
            layer_forward(2)
            layer_finish(0)
        elif k == 18:
            layer_finish(1)
            compute(2, l2, at_left(2))
            compute(2, r2, at_right(2))
        elif k == 19:
            compute(2, l3, at_left(3))
            compute(2, r3, at_right(3))
    z_step(last)
    compute(2, x4, at_left(4))
    last_send()
    layer_finish(2)
    last_finish()

    line = jnp.sum(lanes[...].T, axis=0, keepdims=True)
    line = jnp.broadcast_to(line, (8, 128))
    mytot[...] = line
    for o in range(1, N):
        send(mytot, ctot.at[col], tos.at[o], tor.at[o], {"col": (col + o) % N})
    ctot[col] = line
    sent(len(pending) - (N - 1))
    for o in range(1, N):
        received(ctot.at[(col + N - o) % N], tor.at[o], tos.at[o])
    total = ctot[0]
    for c in range(1, N):
        total += ctot[c]
    scale = jnp.broadcast_to((COLS / total)[0:1], (H, H)).T
    for u in range(8):
        out[:, pl.ds(u * H, H)] *= scale
    sent(len(pending))


def local(left_tiles, left_slots, right_tiles, right_slots):
    bf16, f32, i32 = jnp.bfloat16, jnp.float32, jnp.int32
    dma = pltpu.SemaphoreType.DMA
    block = pltpu.VMEM((CAP_B + 1, T, H), bf16)
    turned = pltpu.VMEM((CAP_B + 1, Q, T), bf16)
    return pl.pallas_call(
        kernel,
        out_shape=pltpu.VMEM((H, 1024), f32),
        in_specs=[
            pl.BlockSpec(memory_space=pl.ANY),
            pl.BlockSpec(memory_space=pl.ANY),
            pl.BlockSpec(memory_space=pl.ANY),
            pl.BlockSpec(memory_space=pl.ANY),
        ],
        out_specs=pl.BlockSpec(memory_space=pltpu.VMEM),
        scratch_shapes=[
            *[block] * 8,
            *[turned] * 16,
            pltpu.VMEM((CAP_B, T, H), bf16),
            pltpu.VMEM((N, CAP_A + 1, T, T), bf16),
            pltpu.VMEM((N, ROW_T * T, KT * T), bf16),
            pltpu.VMEM((2, KT * T, T), bf16),
            pltpu.VMEM((4 * Q, KT * T), bf16),
            pltpu.VMEM((4, 2, 2, H, T), f32),
            pltpu.VMEM((4, 2, H, T), f32),
            pltpu.VMEM((4, H, T), f32),
            pltpu.VMEM((2, H, T), jnp.int16),
            pltpu.VMEM((2, H, T), jnp.int16),
            pltpu.VMEM((H, H), f32),
            pltpu.VMEM((N, 8, 128), i32),
            pltpu.VMEM((N, 8, 128), i32),
            pltpu.SMEM((N, 8, 128), i32),
            pltpu.SMEM((N, 8, 128), i32),
            pltpu.VMEM((8, 128), f32),
            pltpu.VMEM((N, 8, 128), f32),
            dma((2, len(ORDER))), dma((2, len(ORDER))),
            dma((9,)), dma((9,)),
            dma((2, 5)), dma((2, 5)), dma((9,)), dma((9,)), dma((N,)), dma((N,)),
            dma((4,)), dma((4,)), dma((5,)), dma((5,)),
            dma((7,)),
            pltpu.SMEM((CAP_A,), i32),
            pltpu.SMEM((CAP_B,), i32),
        ],
        compiler_params=pltpu.CompilerParams(
            collective_id=0, has_side_effects=True, vmem_limit_bytes=54 * 1024 * 1024
        ),
        cost_estimate=pl.CostEstimate(flops=8_600_000_000, bytes_accessed=2_000_000, transcendentals=0),
    )(
        left_tiles.reshape(CAP_A, T, T),
        left_slots.reshape(CAP_A),
        right_tiles.reshape(CAP_B, T, T),
        right_slots.reshape(CAP_B),
    )


def solution(mesh):
    return jax.shard_map(
        local,
        mesh=mesh,
        in_specs=(
            P("row", "layer", "col", None, None, None),
            P("row", "layer", "col", None),
            P("row", "layer", "col", None, None, None),
            P("row", "layer", "col", None),
        ),
        out_specs=P(("row", "layer"), "col"),
        check_vma=False,
    )
```

```python
import jax
import jax.numpy as jnp
from jax import lax
from jax.experimental import pallas as pl
from jax.experimental.pallas import tpu as pltpu
from jax.sharding import PartitionSpec as P

MESH = pl.DeviceIdType.MESH
T = 256
H = 128
N = 8
CAP_A, CAP_B = 3, 6
KT = 4
COL_T = 4
Q = 64
ROW_T = 2
COLS = 8192
WAYS = (0, 1)
SENT_LATER = 24
LANE_A = 64
HALF = CAP_B // 2
LOWEST, STEPS, ZERO = -6.0, 65534 / 23, -32768
ORDER = [(0, 1, 0), (0, 1, 1), (0, 2, 0), (0, 2, 1), (0, 3, 0), (0, 3, 1), (0, 4, 0)]
ORDER += [(1, 1, 0), (1, 1, 1), (2, 1, 0), (1, 2, 0), (1, 2, 1), (2, 1, 1), (1, 3, 0), (1, 3, 1)]
ORDER += [(2, 2, 0), (2, 2, 1), (1, 4, 0), (2, 3, 0), (2, 3, 1), (2, 4, 0)]


def kernel(
    lt, left_slots, rt, right_slots, out,
    own0, l10, l20, l30, r10, r20, r30, x40,
    own1, l11, l21, l31, r11, r21, r31, x41,
    own2, l12, l22, l32, r12, r22, r32, x42,
    raw,
    abuf, adense, bdense, bturned, acc, in1, in2, coded, incoded, lanes,
    ztab, ctab, zsm, csm, mytot, ctot,
    zs, zr, as_, ar, tzs, tzr, tcs, tcr, tos, tor, s1s, s1r, s2s, s2r, loc, ls, rs,
):
    row = lax.axis_index("row")
    col = lax.axis_index("col")
    layer = lax.axis_index("layer")
    core, ylo = layer % 2, layer // 2
    pending = []
    own, x4 = (own0, own1, own2), (x40, x41, x42)
    l1, l2, l3 = (l10, l11, l12), (l20, l21, l22), (l30, l31, l32)
    r1, r2, r3 = (r10, r11, r12), (r20, r21, r22), (r30, r31, r32)

    def send(src, dst, ss, rs_, device):
        copy = pltpu.make_async_remote_copy(
            src_ref=src, dst_ref=dst, send_sem=ss, recv_sem=rs_, device_id=device, device_id_type=MESH
        )
        copy.start()
        pending.append(copy)

    def sent(count):
        for copy in pending[: max(count, 0)]:
            copy.wait_send()
        del pending[: max(count, 0)]

    def received(dst, rs_, ss):
        pltpu.make_async_remote_copy(
            src_ref=dst, dst_ref=dst, send_sem=ss, recv_sem=rs_, device_id={"row": (row + 1) % N}, device_id_type=MESH
        ).wait_recv()

    core_peer = {"layer": ylo * 2 + (1 - core)}
    y_peer = {"layer": (1 - ylo) * 2 + core}
    right, left = {"row": (row + 1) % N}, {"row": (row + N - 1) % N}
    xright, xleft = {"col": (col + 2) % N}, {"col": (col + N - 2) % N}
    ypair_col = col + 1 - 2 * (col % 2)
    ypair = {"col": ypair_col}
    peers = [right, left, xright, xleft, ypair, core_peer, y_peer]
    barrier = pltpu.get_barrier_semaphore()
    for peer in peers:
        pl.semaphore_signal(barrier, inc=1, device_id=peer, device_id_type=MESH)

    local = [pltpu.make_async_copy(lt, abuf.at[col, pl.ds(0, CAP_A)], loc.at[0])]
    local.append(pltpu.make_async_copy(rt.at[:, :, pl.ds(0, H)], own0.at[pl.ds(0, CAP_B)], loc.at[1]))
    local.append(pltpu.make_async_copy(rt.at[:, :, pl.ds(H, H)], raw, loc.at[2]))
    local.append(pltpu.make_async_copy(left_slots, ls, loc.at[5]))
    local.append(pltpu.make_async_copy(right_slots, rs, loc.at[6]))
    for copy in local:
        copy.start()
    pl.semaphore_wait(barrier, len(peers))

    from_left = [None, l1, l2, l3, x4]
    from_right = [None, r1, r2, r3, x4]

    def z_send(k, way):
        held, device = ((from_left, right), (from_right, left))[way]
        p, d, q = ORDER[k]
        piece = pl.ds((q if way == 0 else 1 - q) * HALF, HALF)
        if d > 1:
            src = held[d - 1][p].at[piece]
        elif p == 0:
            src = rt.at[piece, :, pl.ds(0, H)]
        else:
            src = own[p].at[piece]
        send(src, held[d][p].at[piece], zs.at[way, k], zr.at[way, k], device)

    def z_step(k):
        for way in WAYS:
            p, d, q = ORDER[k]
            piece = pl.ds((q if way == 0 else 1 - q) * HALF, HALF)
            received((from_left, from_right)[way][d][p].at[piece], zr.at[way, k], zs.at[way, k])
            while started[way] < len(ORDER):
                j = started[way]
                p, d, q = ORDER[j]
                if j - k > (2 if p == 0 else 4) or (d > 1 and ORDER.index((p, d - 1, q)) > k):
                    break
                started[way] += 1
                z_send(j, way)

    def z_table(d):
        if d > 1:
            received(ztab.at[(row + N - d + 1) % N], tzr.at[0, d - 1], tzs.at[0, d - 1])
            received(ztab.at[(row + d - 1) % N], tzr.at[1, d - 1], tzs.at[1, d - 1])
        lines = ztab.at[(row + N - d + 1) % N]
        send(lines, lines, tzs.at[0, d], tzr.at[0, d], right)
        if d < 4:
            lines = ztab.at[(row + d - 1) % N]
            send(lines, lines, tzs.at[1, d], tzr.at[1, d], left)

    def a_table(i, block, device):
        send(ctab.at[block], ctab.at[block], tcs.at[i], tcr.at[i], device)

    def a_table_received(i, block):
        received(ctab.at[block], tcr.at[i], tcs.at[i])

    def a_send(i, block, part, device):
        ref = abuf.at[block, pl.ds(0, CAP_A)] if part is None else abuf.at[block, pl.ds(0, CAP_A), pl.ds(part * H, H)]
        send(ref, ref, as_.at[i], ar.at[i], device)

    def a_received(i, block, part):
        ref = abuf.at[block, pl.ds(0, CAP_A)] if part is None else abuf.at[block, pl.ds(0, CAP_A), pl.ds(part * H, H)]
        received(ref, ar.at[i], as_.at[i])

    def a_first(base, block):
        a_send(base, block, None, xright)
        a_send(base + 1, block, None, xleft)
        a_table(base, block, xright)
        a_table(base + 1, block, xleft)

    def a_forward(base, block):
        a_received(base, (block + N - 2) % N, None)
        a_send(base + 2, (block + N - 2) % N, 0, xright)
        a_table_received(base, (block + N - 2) % N)
        a_table(base + 2, (block + N - 2) % N, xright)
        a_received(base + 1, (block + 2) % N, None)
        a_send(base + 3, (block + 2) % N, 1, xleft)
        a_table_received(base + 1, (block + 2) % N)

    def a_last(base, block):
        a_received(base + 2, (block + 4) % N, 0)
        a_received(base + 3, (block + 4) % N, 1)
        a_table_received(base + 2, (block + 4) % N)

    started = [2, 2]
    for way in WAYS:
        z_send(0, way)
        z_send(1, way)
    for ref in (own, l1, l2, l3, r1, r2, r3, x4):
        ref[0][CAP_B] = jnp.zeros((T, H), jnp.bfloat16)
        for p in (1, 2):
            ref[p][CAP_B] = jnp.zeros((Q, T), jnp.bfloat16)
    for c in range(N):
        abuf[c, CAP_A] = jnp.zeros((T, T), jnp.bfloat16)

    low = lax.broadcasted_iota(jnp.int32, (H, H), 1) < Q
    lane = lax.broadcasted_iota(jnp.int32, (8, 128), 1)
    table = jnp.where(lane < LANE_A, CAP_B, CAP_A)
    local[3].wait()
    local[4].wait()
    for s in range(CAP_B):
        table = jnp.where(lane == rs[s], s, table)
    for s in range(CAP_A):
        table = jnp.where(lane == ls[s] + LANE_A, s, table)
    ztab[row] = table
    ctab[col] = table
    local[0].wait()
    a_send(8, col, None, ypair)
    a_table(8, col, ypair)
    a_first(0, col)
    z_table(1)
    acc[...] = jnp.zeros_like(acc)
    lanes[...] = jnp.zeros_like(lanes)
    local[1].wait()
    local[2].wait()
    for tile in range(CAP_B):
        turned = raw[tile].T
        own1[tile] = turned[:Q]
        own2[tile] = turned[Q:]

    def tables():
        received(ztab.at[(row + 4) % N], tzr.at[0, 4], tzs.at[0, 4])
        c1 = pltpu.make_async_copy(ztab, zsm, loc.at[3])
        c2 = pltpu.make_async_copy(ctab, csm, loc.at[4])
        c1.start()
        c2.start()
        c1.wait()
        c2.wait()

    def densify_a(first, last):
        def body(c, carry):
            for i in range(ROW_T):
                for kk in range(KT):
                    s = csm[c, 0, LANE_A + i * KT + kk]
                    adense[c, pl.ds(i * T, T), pl.ds(kk * T, T)] = abuf[c, s]
            return carry

        lax.fori_loop(first, last, body, 0)

    def compute(p, ref, j, after=None):
        for kk in range(KT):
            for jc in range(COL_T):
                s = zsm[j, 0, kk * COL_T + jc]
                if p == 0:
                    bdense[jc // 2, pl.ds(kk * T, T), pl.ds((jc % 2) * H, H)] = ref[p][s]
                else:
                    bturned[pl.ds(jc * Q, Q), pl.ds(kk * T, T)] = ref[p][s]
        for n in range(2) if p == 0 else (p + 1,):
            for i in range(ROW_T):
                rows = adense[j, pl.ds(i * T, T)]
                if p == 0:
                    part = jnp.dot(rows, bdense[n], preferred_element_type=jnp.float32)
                else:
                    part = lax.dot_general(
                        rows, bturned[...], (((1,), (1,)), ((), ())), preferred_element_type=jnp.float32
                    )
                acc[n, 0, i] += part[:H]
                acc[n, 1, i] += part[H:]
            if after is not None:
                after(n)

    def layer_send(n):
        send(acc.at[n, 1 - core], in1.at[n], s1s.at[n], s1r.at[n], core_peer)

    def layer_forward(n):
        received(in1.at[n], s1r.at[n], s1s.at[n])
        acc[n, core, 1 - ylo] += in1[n, 1 - ylo]
        send(acc.at[n, core, 1 - ylo], in2.at[n], s2s.at[n], s2r.at[n], y_peer)

    def layer_finish(n):
        received(in2.at[n], s2r.at[n], s2s.at[n])
        finish(n, acc[n, core, ylo] + in1[n, ylo] + in2[n])

    def finish(n, total):
        squares = total * total
        lanes[...] += squares[:, :H] + squares[:, H:]
        for u in range(2):
            part = squares[:, u * H : (u + 1) * H]
            if n < 2:
                out[:, pl.ds((n * 2 + u) * T, H)] = part
                continue
            turned = pltpu.roll(part, Q, 1)
            for v in range(2):
                place = pl.ds((u * 2 + v) * T + H, H)
                if n == 2:
                    out[:, place] = turned if v else part
                else:
                    out[:, place] = jnp.where(low, out[:, place], part if v else turned)

    def code(v):
        steps = (jnp.log2(jnp.maximum(v, 2.0**LOWEST)) - LOWEST) * STEPS
        steps = jnp.minimum(jnp.round(steps), 65534.0) - 32767.0
        return jnp.where(v > 0, steps, float(ZERO)).astype(jnp.int32).astype(jnp.int16)

    def decode(q):
        steps = q.astype(jnp.int32).astype(jnp.float32)
        v = jnp.exp2((steps + 32767.0) * (1.0 / STEPS) + LOWEST)
        return jnp.where(steps > ZERO + 0.5, v, 0.0)

    def across(c):
        return {"layer": (1 - ylo) * 2 + c}

    def last_send():
        send(acc.at[3, 1 - core, ylo], in1.at[3, 0], s1s.at[3], s1r.at[3], core_peer)
        for u in range(2):
            c = core if u else 1 - core
            coded[u] = code(acc[3, c, 1 - ylo])
            send(coded.at[u], incoded.at[core], s2s.at[3 + u], s2r.at[3 + u], across(c))

    def last_finish():
        received(in1.at[3, 0], s1r.at[3], s1s.at[3])
        total = acc[3, core, ylo] + in1[3, 0]
        for u in range(2):
            c = core if u else 1 - core
            received(incoded.at[c], s2r.at[3 + u], s2s.at[3 + u])
            total += decode(incoded[c])
        finish(3, total)

    def at_left(d):
        return (row + N - d) % N

    def at_right(d):
        return (row + d) % N

    last = len(ORDER) - 1
    for k in range(last):
        z_step(k)
        if k >= 3:
            sent(len(pending) - SENT_LATER)
        if k == 0:
            z_table(2)
        elif k == 1:
            z_table(3)
        elif k == 2:
            z_table(4)
            a_forward(0, col)
            a_received(8, ypair_col, None)
            a_table_received(8, ypair_col)
            a_first(4, ypair_col)
        elif k == 4:
            a_last(0, col)
        elif k == 5:
            a_forward(4, ypair_col)
        elif k == 8:
            a_last(4, ypair_col)
            tables()
            densify_a(0, N // 2)
        elif k == 9:
            densify_a(N // 2, N)
        elif k == 10:
            compute(0, own, row)
            compute(0, l1, at_left(1))
        elif k == 11:
            compute(0, r1, at_right(1))
            compute(0, l2, at_left(2))
        elif k == 12:
            compute(0, r2, at_right(2))
            compute(0, l3, at_left(3))
        elif k == 13:
            compute(0, r3, at_right(3))
            compute(0, x4, at_left(4), layer_send)
        elif k == 14:
            compute(1, own, row)
            compute(1, l1, at_left(1))
            compute(1, r1, at_right(1))
            layer_forward(0)
            layer_forward(1)
        elif k == 15:
            compute(1, l2, at_left(2))
            compute(1, r2, at_right(2))
            compute(1, l3, at_left(3))
            compute(1, r3, at_right(3))
        elif k == 16:
            compute(2, own, row)
            compute(2, l1, at_left(1))
            compute(2, r1, at_right(1))
            compute(2, l2, at_left(2))
            compute(2, r2, at_right(2))
        elif k == 17:
            compute(1, x4, at_left(4), layer_send)
            layer_finish(0)
        elif k == 18:
            layer_forward(2)
            layer_finish(1)
        elif k == 19:
            compute(2, l3, at_left(3))
            compute(2, r3, at_right(3))
    z_step(last)
    compute(2, x4, at_left(4))
    last_send()
    layer_finish(2)
    last_finish()

    line = jnp.sum(lanes[...].T, axis=0, keepdims=True)
    line = jnp.broadcast_to(line, (8, 128))
    mytot[...] = line
    for o in range(1, N):
        send(mytot, ctot.at[col], tos.at[o], tor.at[o], {"col": (col + o) % N})
    ctot[col] = line
    sent(len(pending) - (N - 1))
    for o in range(1, N):
        received(ctot.at[(col + N - o) % N], tor.at[o], tos.at[o])
    total = ctot[0]
    for c in range(1, N):
        total += ctot[c]
    scale = jnp.broadcast_to((COLS / total)[0:1], (H, H)).T
    for u in range(8):
        out[:, pl.ds(u * H, H)] *= scale
    sent(len(pending))


def local(left_tiles, left_slots, right_tiles, right_slots):
    bf16, f32, i32 = jnp.bfloat16, jnp.float32, jnp.int32
    dma = pltpu.SemaphoreType.DMA
    block = pltpu.VMEM((CAP_B + 1, T, H), bf16)
    turned = pltpu.VMEM((CAP_B + 1, Q, T), bf16)
    return pl.pallas_call(
        kernel,
        out_shape=pltpu.VMEM((H, 1024), f32),
        in_specs=[
            pl.BlockSpec(memory_space=pl.ANY),
            pl.BlockSpec(memory_space=pl.ANY),
            pl.BlockSpec(memory_space=pl.ANY),
            pl.BlockSpec(memory_space=pl.ANY),
        ],
        out_specs=pl.BlockSpec(memory_space=pltpu.VMEM),
        scratch_shapes=[
            *[block] * 8,
            *[turned] * 16,
            pltpu.VMEM((CAP_B, T, H), bf16),
            pltpu.VMEM((N, CAP_A + 1, T, T), bf16),
            pltpu.VMEM((N, ROW_T * T, KT * T), bf16),
            pltpu.VMEM((2, KT * T, T), bf16),
            pltpu.VMEM((4 * Q, KT * T), bf16),
            pltpu.VMEM((4, 2, 2, H, T), f32),
            pltpu.VMEM((4, 2, H, T), f32),
            pltpu.VMEM((4, H, T), f32),
            pltpu.VMEM((2, H, T), jnp.int16),
            pltpu.VMEM((2, H, T), jnp.int16),
            pltpu.VMEM((H, H), f32),
            pltpu.VMEM((N, 8, 128), i32),
            pltpu.VMEM((N, 8, 128), i32),
            pltpu.SMEM((N, 8, 128), i32),
            pltpu.SMEM((N, 8, 128), i32),
            pltpu.VMEM((8, 128), f32),
            pltpu.VMEM((N, 8, 128), f32),
            dma((2, len(ORDER))), dma((2, len(ORDER))),
            dma((9,)), dma((9,)),
            dma((2, 5)), dma((2, 5)), dma((9,)), dma((9,)), dma((N,)), dma((N,)),
            dma((4,)), dma((4,)), dma((5,)), dma((5,)),
            dma((7,)),
            pltpu.SMEM((CAP_A,), i32),
            pltpu.SMEM((CAP_B,), i32),
        ],
        compiler_params=pltpu.CompilerParams(
            collective_id=0, has_side_effects=True, vmem_limit_bytes=54 * 1024 * 1024
        ),
        cost_estimate=pl.CostEstimate(flops=8_600_000_000, bytes_accessed=2_000_000, transcendentals=0),
    )(
        left_tiles.reshape(CAP_A, T, T),
        left_slots.reshape(CAP_A),
        right_tiles.reshape(CAP_B, T, T),
        right_slots.reshape(CAP_B),
    )


def solution(mesh):
    return jax.shard_map(
        local,
        mesh=mesh,
        in_specs=(
            P("row", "layer", "col", None, None, None),
            P("row", "layer", "col", None),
            P("row", "layer", "col", None, None, None),
            P("row", "layer", "col", None),
        ),
        out_specs=P(("row", "layer"), "col"),
        check_vma=False,
    )
```

```python
import jax
import jax.numpy as jnp
from jax import lax
from jax.experimental import pallas as pl
from jax.experimental.pallas import tpu as pltpu
from jax.sharding import PartitionSpec as P

MESH = pl.DeviceIdType.MESH
T = 256
H = 128
N = 8
CAP_A, CAP_B = 3, 6
KT = 4
COL_T = 4
Q = 64
ROW_T = 2
COLS = 8192
WAYS = (0, 1)
SENT_LATER = 24
LANE_A = 64
HALF = CAP_B // 2
LOWEST, STEPS, ZERO = -6.0, 65534 / 23, -32768
ORDER = [(0, 1, 0), (0, 1, 1), (0, 2, 0), (0, 2, 1), (0, 3, 0), (0, 3, 1), (0, 4, 0)]
ORDER += [(1, 1, 0), (1, 1, 1), (2, 1, 0), (1, 2, 0), (1, 2, 1), (2, 1, 1), (1, 3, 0), (1, 3, 1)]
ORDER += [(2, 2, 0), (2, 2, 1), (1, 4, 0), (2, 3, 0), (2, 3, 1), (2, 4, 0)]


def kernel(
    lt, left_slots, rt, right_slots, out,
    own0, l10, l20, l30, r10, r20, r30, x40,
    own1, l11, l21, l31, r11, r21, r31, x41,
    own2, l12, l22, l32, r12, r22, r32, x42,
    raw,
    abuf, adense, bdense, bturned, acc, in1, in2, coded, incoded, lanes,
    ztab, ctab, zsm, csm, mytot, ctot,
    zs, zr, as_, ar, tzs, tzr, tcs, tcr, tos, tor, s1s, s1r, s2s, s2r, loc, ls, rs,
):
    row = lax.axis_index("row")
    col = lax.axis_index("col")
    layer = lax.axis_index("layer")
    core, ylo = layer % 2, layer // 2
    pending = []
    own, x4 = (own0, own1, own2), (x40, x41, x42)
    l1, l2, l3 = (l10, l11, l12), (l20, l21, l22), (l30, l31, l32)
    r1, r2, r3 = (r10, r11, r12), (r20, r21, r22), (r30, r31, r32)

    def send(src, dst, ss, rs_, device):
        copy = pltpu.make_async_remote_copy(
            src_ref=src, dst_ref=dst, send_sem=ss, recv_sem=rs_, device_id=device, device_id_type=MESH
        )
        copy.start()
        pending.append(copy)

    def sent(count):
        for copy in pending[: max(count, 0)]:
            copy.wait_send()
        del pending[: max(count, 0)]

    def received(dst, rs_, ss):
        pltpu.make_async_remote_copy(
            src_ref=dst, dst_ref=dst, send_sem=ss, recv_sem=rs_, device_id={"row": (row + 1) % N}, device_id_type=MESH
        ).wait_recv()

    core_peer = {"layer": ylo * 2 + (1 - core)}
    y_peer = {"layer": (1 - ylo) * 2 + core}
    right, left = {"row": (row + 1) % N}, {"row": (row + N - 1) % N}
    xright, xleft = {"col": (col + 2) % N}, {"col": (col + N - 2) % N}
    ypair_col = col + 1 - 2 * (col % 2)
    ypair = {"col": ypair_col}
    peers = [right, left, xright, xleft, ypair, core_peer, y_peer]
    barrier = pltpu.get_barrier_semaphore()
    for peer in peers:
        pl.semaphore_signal(barrier, inc=1, device_id=peer, device_id_type=MESH)

    local = [pltpu.make_async_copy(lt, abuf.at[col, pl.ds(0, CAP_A)], loc.at[0])]
    local.append(pltpu.make_async_copy(rt.at[:, :, pl.ds(0, H)], own0.at[pl.ds(0, CAP_B)], loc.at[1]))
    local.append(pltpu.make_async_copy(rt.at[:, :, pl.ds(H, H)], raw, loc.at[2]))
    local.append(pltpu.make_async_copy(left_slots, ls, loc.at[5]))
    local.append(pltpu.make_async_copy(right_slots, rs, loc.at[6]))
    for copy in local:
        copy.start()
    pl.semaphore_wait(barrier, len(peers))

    from_left = [None, l1, l2, l3, x4]
    from_right = [None, r1, r2, r3, x4]

    def z_send(k, way):
        held, device = ((from_left, right), (from_right, left))[way]
        p, d, q = ORDER[k]
        piece = pl.ds((q if way == 0 else 1 - q) * HALF, HALF)
        if d > 1:
            src = held[d - 1][p].at[piece]
        elif p == 0:
            src = rt.at[piece, :, pl.ds(0, H)]
        else:
            src = own[p].at[piece]
        send(src, held[d][p].at[piece], zs.at[way, k], zr.at[way, k], device)

    def z_step(k):
        for way in WAYS:
            p, d, q = ORDER[k]
            piece = pl.ds((q if way == 0 else 1 - q) * HALF, HALF)
            received((from_left, from_right)[way][d][p].at[piece], zr.at[way, k], zs.at[way, k])
            while started[way] < len(ORDER):
                j = started[way]
                p, d, q = ORDER[j]
                if j - k > (2 if p == 0 else 4) or (d > 1 and ORDER.index((p, d - 1, q)) > k):
                    break
                started[way] += 1
                z_send(j, way)

    def z_table(d):
        if d > 1:
            received(ztab.at[(row + N - d + 1) % N], tzr.at[0, d - 1], tzs.at[0, d - 1])
            received(ztab.at[(row + d - 1) % N], tzr.at[1, d - 1], tzs.at[1, d - 1])
        lines = ztab.at[(row + N - d + 1) % N]
        send(lines, lines, tzs.at[0, d], tzr.at[0, d], right)
        if d < 4:
            lines = ztab.at[(row + d - 1) % N]
            send(lines, lines, tzs.at[1, d], tzr.at[1, d], left)

    def a_table(i, block, device):
        send(ctab.at[block], ctab.at[block], tcs.at[i], tcr.at[i], device)

    def a_table_received(i, block):
        received(ctab.at[block], tcr.at[i], tcs.at[i])

    def a_send(i, block, part, device):
        ref = abuf.at[block, pl.ds(0, CAP_A)] if part is None else abuf.at[block, pl.ds(0, CAP_A), pl.ds(part * H, H)]
        send(ref, ref, as_.at[i], ar.at[i], device)

    def a_received(i, block, part):
        ref = abuf.at[block, pl.ds(0, CAP_A)] if part is None else abuf.at[block, pl.ds(0, CAP_A), pl.ds(part * H, H)]
        received(ref, ar.at[i], as_.at[i])

    def a_first(base, block):
        a_send(base, block, None, xright)
        a_send(base + 1, block, None, xleft)
        a_table(base, block, xright)
        a_table(base + 1, block, xleft)

    def a_forward(base, block):
        a_received(base, (block + N - 2) % N, None)
        a_send(base + 2, (block + N - 2) % N, 0, xright)
        a_table_received(base, (block + N - 2) % N)
        a_table(base + 2, (block + N - 2) % N, xright)
        a_received(base + 1, (block + 2) % N, None)
        a_send(base + 3, (block + 2) % N, 1, xleft)
        a_table_received(base + 1, (block + 2) % N)

    def a_last(base, block):
        a_received(base + 2, (block + 4) % N, 0)
        a_received(base + 3, (block + 4) % N, 1)
        a_table_received(base + 2, (block + 4) % N)

    started = [2, 2]
    for way in WAYS:
        z_send(0, way)
        z_send(1, way)
    for ref in (own, l1, l2, l3, r1, r2, r3, x4):
        ref[0][CAP_B] = jnp.zeros((T, H), jnp.bfloat16)
        for p in (1, 2):
            ref[p][CAP_B] = jnp.zeros((Q, T), jnp.bfloat16)
    for c in range(N):
        abuf[c, CAP_A] = jnp.zeros((T, T), jnp.bfloat16)

    low = lax.broadcasted_iota(jnp.int32, (H, H), 1) < Q
    lane = lax.broadcasted_iota(jnp.int32, (8, 128), 1)
    table = jnp.where(lane < LANE_A, CAP_B, CAP_A)
    local[3].wait()
    local[4].wait()
    for s in range(CAP_B):
        table = jnp.where(lane == rs[s], s, table)
    for s in range(CAP_A):
        table = jnp.where(lane == ls[s] + LANE_A, s, table)
    ztab[row] = table
    ctab[col] = table
    local[0].wait()
    a_send(8, col, None, ypair)
    a_table(8, col, ypair)
    a_first(0, col)
    z_table(1)
    acc[...] = jnp.zeros_like(acc)
    lanes[...] = jnp.zeros_like(lanes)
    local[1].wait()
    local[2].wait()
    for tile in range(CAP_B):
        turned = raw[tile].T
        own1[tile] = turned[:Q]
        own2[tile] = turned[Q:]

    def tables():
        received(ztab.at[(row + 4) % N], tzr.at[0, 4], tzs.at[0, 4])
        c1 = pltpu.make_async_copy(ztab, zsm, loc.at[3])
        c2 = pltpu.make_async_copy(ctab, csm, loc.at[4])
        c1.start()
        c2.start()
        c1.wait()
        c2.wait()

    def densify_a(first, last):
        def body(c, carry):
            for i in range(ROW_T):
                for kk in range(KT):
                    s = csm[c, 0, LANE_A + i * KT + kk]
                    adense[c, pl.ds(i * T, T), pl.ds(kk * T, T)] = abuf[c, s]
            return carry

        lax.fori_loop(first, last, body, 0)

    def compute(p, ref, j, after=None):
        for kk in range(KT):
            for jc in range(COL_T):
                s = zsm[j, 0, kk * COL_T + jc]
                if p == 0:
                    bdense[jc // 2, pl.ds(kk * T, T), pl.ds((jc % 2) * H, H)] = ref[p][s]
                else:
                    bturned[pl.ds(jc * Q, Q), pl.ds(kk * T, T)] = ref[p][s]
        for n in range(2) if p == 0 else (p + 1,):
            for i in range(ROW_T):
                rows = adense[j, pl.ds(i * T, T)]
                if p == 0:
                    part = jnp.dot(rows, bdense[n], preferred_element_type=jnp.float32)
                else:
                    part = lax.dot_general(
                        rows, bturned[...], (((1,), (1,)), ((), ())), preferred_element_type=jnp.float32
                    )
                acc[n, 0, i] += part[:H]
                acc[n, 1, i] += part[H:]
            if after is not None:
                after(n)

    def layer_send(n):
        send(acc.at[n, 1 - core], in1.at[n], s1s.at[n], s1r.at[n], core_peer)

    def layer_forward(n):
        received(in1.at[n], s1r.at[n], s1s.at[n])
        acc[n, core, 1 - ylo] += in1[n, 1 - ylo]
        send(acc.at[n, core, 1 - ylo], in2.at[n], s2s.at[n], s2r.at[n], y_peer)

    def layer_finish(n):
        received(in2.at[n], s2r.at[n], s2s.at[n])
        finish(n, acc[n, core, ylo] + in1[n, ylo] + in2[n])

    def finish(n, total):
        squares = total * total
        lanes[...] += squares[:, :H] + squares[:, H:]
        for u in range(2):
            part = squares[:, u * H : (u + 1) * H]
            if n < 2:
                out[:, pl.ds((n * 2 + u) * T, H)] = part
                continue
            turned = pltpu.roll(part, Q, 1)
            for v in range(2):
                place = pl.ds((u * 2 + v) * T + H, H)
                if n == 2:
                    out[:, place] = turned if v else part
                else:
                    out[:, place] = jnp.where(low, out[:, place], part if v else turned)

    def code(v):
        steps = (jnp.log2(jnp.maximum(v, 2.0**LOWEST)) - LOWEST) * STEPS
        steps = jnp.minimum(jnp.round(steps), 65534.0) - 32767.0
        return jnp.where(v > 0, steps, float(ZERO)).astype(jnp.int32).astype(jnp.int16)

    def decode(q):
        steps = q.astype(jnp.int32).astype(jnp.float32)
        v = jnp.exp2((steps + 32767.0) * (1.0 / STEPS) + LOWEST)
        return jnp.where(steps > ZERO + 0.5, v, 0.0)

    def across(c):
        return {"layer": (1 - ylo) * 2 + c}

    def last_rows(j, i):
        rows = adense[j, pl.ds(pl.multiple_of(i * T, T), T)]
        part = lax.dot_general(
            rows, bturned[...], (((1,), (1,)), ((), ())), preferred_element_type=jnp.float32
        )
        acc[3, 0, i] += part[:H]
        acc[3, 1, i] += part[H:]

    def last_compute(j):
        for kk in range(KT):
            for jc in range(COL_T):
                bturned[pl.ds(jc * Q, Q), pl.ds(kk * T, T)] = x4[2][zsm[j, 0, kk * COL_T + jc]]
        last_rows(j, 1 - ylo)
        for u in range(2):
            c = core if u else 1 - core
            coded[u] = code(acc[3, c, 1 - ylo])
            send(coded.at[u], incoded.at[core], s2s.at[3 + u], s2r.at[3 + u], across(c))
        last_rows(j, ylo)
        send(acc.at[3, 1 - core, ylo], in1.at[3, 0], s1s.at[3], s1r.at[3], core_peer)

    def last_finish():
        received(in1.at[3, 0], s1r.at[3], s1s.at[3])
        total = acc[3, core, ylo] + in1[3, 0]
        for u in range(2):
            c = core if u else 1 - core
            received(incoded.at[c], s2r.at[3 + u], s2s.at[3 + u])
            total += decode(incoded[c])
        finish(3, total)

    def at_left(d):
        return (row + N - d) % N

    def at_right(d):
        return (row + d) % N

    last = len(ORDER) - 1
    for k in range(last):
        z_step(k)
        if k >= 3:
            sent(len(pending) - SENT_LATER)
        if k == 0:
            z_table(2)
        elif k == 1:
            z_table(3)
        elif k == 2:
            z_table(4)
            a_forward(0, col)
            a_received(8, ypair_col, None)
            a_table_received(8, ypair_col)
            a_first(4, ypair_col)
        elif k == 4:
            a_last(0, col)
        elif k == 5:
            a_forward(4, ypair_col)
        elif k == 8:
            a_last(4, ypair_col)
            tables()
            densify_a(0, N // 2)
        elif k == 9:
            densify_a(N // 2, N)
        elif k == 10:
            compute(0, own, row)
            compute(0, l1, at_left(1))
        elif k == 11:
            compute(0, r1, at_right(1))
            compute(0, l2, at_left(2))
        elif k == 12:
            compute(0, r2, at_right(2))
            compute(0, l3, at_left(3))
        elif k == 13:
            compute(0, r3, at_right(3))
            compute(0, x4, at_left(4), layer_send)
        elif k == 14:
            compute(1, own, row)
            compute(1, l1, at_left(1))
            compute(1, r1, at_right(1))
            layer_forward(0)
            layer_forward(1)
        elif k == 15:
            compute(1, l2, at_left(2))
            compute(1, r2, at_right(2))
            compute(1, l3, at_left(3))
            compute(1, r3, at_right(3))
        elif k == 16:
            compute(2, own, row)
            compute(2, l1, at_left(1))
            compute(2, r1, at_right(1))
            compute(2, l2, at_left(2))
            compute(2, r2, at_right(2))
        elif k == 17:
            compute(1, x4, at_left(4), layer_send)
            layer_finish(0)
        elif k == 18:
            layer_forward(2)
            layer_finish(1)
        elif k == 19:
            compute(2, l3, at_left(3))
            compute(2, r3, at_right(3))
    z_step(last)
    last_compute(at_left(4))
    layer_finish(2)
    last_finish()

    line = jnp.sum(lanes[...].T, axis=0, keepdims=True)
    line = jnp.broadcast_to(line, (8, 128))
    mytot[...] = line
    for o in range(1, N):
        send(mytot, ctot.at[col], tos.at[o], tor.at[o], {"col": (col + o) % N})
    ctot[col] = line
    sent(len(pending) - (N - 1))
    for o in range(1, N):
        received(ctot.at[(col + N - o) % N], tor.at[o], tos.at[o])
    total = ctot[0]
    for c in range(1, N):
        total += ctot[c]
    scale = jnp.broadcast_to((COLS / total)[0:1], (H, H)).T
    for u in range(8):
        out[:, pl.ds(u * H, H)] *= scale
    sent(len(pending))


def local(left_tiles, left_slots, right_tiles, right_slots):
    bf16, f32, i32 = jnp.bfloat16, jnp.float32, jnp.int32
    dma = pltpu.SemaphoreType.DMA
    block = pltpu.VMEM((CAP_B + 1, T, H), bf16)
    turned = pltpu.VMEM((CAP_B + 1, Q, T), bf16)
    return pl.pallas_call(
        kernel,
        out_shape=pltpu.VMEM((H, 1024), f32),
        in_specs=[
            pl.BlockSpec(memory_space=pl.ANY),
            pl.BlockSpec(memory_space=pl.ANY),
            pl.BlockSpec(memory_space=pl.ANY),
            pl.BlockSpec(memory_space=pl.ANY),
        ],
        out_specs=pl.BlockSpec(memory_space=pltpu.VMEM),
        scratch_shapes=[
            *[block] * 8,
            *[turned] * 16,
            pltpu.VMEM((CAP_B, T, H), bf16),
            pltpu.VMEM((N, CAP_A + 1, T, T), bf16),
            pltpu.VMEM((N, ROW_T * T, KT * T), bf16),
            pltpu.VMEM((2, KT * T, T), bf16),
            pltpu.VMEM((4 * Q, KT * T), bf16),
            pltpu.VMEM((4, 2, 2, H, T), f32),
            pltpu.VMEM((4, 2, H, T), f32),
            pltpu.VMEM((4, H, T), f32),
            pltpu.VMEM((2, H, T), jnp.int16),
            pltpu.VMEM((2, H, T), jnp.int16),
            pltpu.VMEM((H, H), f32),
            pltpu.VMEM((N, 8, 128), i32),
            pltpu.VMEM((N, 8, 128), i32),
            pltpu.SMEM((N, 8, 128), i32),
            pltpu.SMEM((N, 8, 128), i32),
            pltpu.VMEM((8, 128), f32),
            pltpu.VMEM((N, 8, 128), f32),
            dma((2, len(ORDER))), dma((2, len(ORDER))),
            dma((9,)), dma((9,)),
            dma((2, 5)), dma((2, 5)), dma((9,)), dma((9,)), dma((N,)), dma((N,)),
            dma((4,)), dma((4,)), dma((5,)), dma((5,)),
            dma((7,)),
            pltpu.SMEM((CAP_A,), i32),
            pltpu.SMEM((CAP_B,), i32),
        ],
        compiler_params=pltpu.CompilerParams(
            collective_id=0, has_side_effects=True, vmem_limit_bytes=54 * 1024 * 1024
        ),
        cost_estimate=pl.CostEstimate(flops=8_600_000_000, bytes_accessed=2_000_000, transcendentals=0),
    )(
        left_tiles.reshape(CAP_A, T, T),
        left_slots.reshape(CAP_A),
        right_tiles.reshape(CAP_B, T, T),
        right_slots.reshape(CAP_B),
    )


def solution(mesh):
    return jax.shard_map(
        local,
        mesh=mesh,
        in_specs=(
            P("row", "layer", "col", None, None, None),
            P("row", "layer", "col", None),
            P("row", "layer", "col", None, None, None),
            P("row", "layer", "col", None),
        ),
        out_specs=P(("row", "layer"), "col"),
        check_vma=False,
    )
```
